32 devices in a mesh: groups: 2 (over x), node: 16 (over z, y, core).
Axes of the slice: x: 2, y: 2, z: 4, core: 2. Of those that a mesh axis runs over, the one named last changes fastest.
Arguments:
- child_query: bfloat16 [3072, 64, 576], P(('groups', 'node')), parts along dimension 0, may hold values from -24 to 24
- parent_cache: bfloat16 [32, 384, 576], P(('groups', 'node')), parts along dimension 0, may hold values from -4 to 4
- child_latent: bfloat16 [3072, 576], P(('groups', 'node')), parts along dimension 0, may hold values from -4 to 4
- parent_place: int32 [32], P('groups'), parts along dimension 0, may hold values from 0 to 15, each once
- child_parent: int32 [3072, 1], P(('groups', 'node')), parts along dimension 0, may hold values from 0 to 15; in each aligned block of 96 rows (0 to 95, 96 to 191, ...) at most 12 rows name the same one
- live_rows: int32 [32], P(('groups', 'node')), parts along dimension 0, may hold values from 72 to 96, as said below
Outputs:
- attended: bfloat16 [3072, 64, 512], P(('groups', 'node')), parts along dimension 0
The draws below stay inside these ranges and needn't reach their ends.
There are 2 independent parts, one for each index of `groups`. The reference program is written for one: setup_inputs(seed, part) draws one part's arguments, and reference() takes and returns one part's arrays. A program takes and returns all parts, laid end to end along the dimension named above; each array names one. Nothing has to cross between parts.
Inputs may be any that keep to these rules, and one draw needn't show every extreme that they name: `child_parent`: within the rows of one device at most 12 rows name the same parent, and some device has exactly 12 rows naming one parent. `live_rows`: some device has all 96 slots live.
All inputs are finite; a program needn't handle non-finite values.
Results may differ from the reference program's by a relative error of at most 0.0047.
Values may be sent and summed in bfloat16 or wider, within the bound.
No kernel may reach another device: no remote copies, remote signals or barrier semaphores. Data moves between devices by JAX's collectives and lax.ppermute only.
A program may use at most 192 MiB of HBM per device.

```python
import math
import jax
import jax.numpy as jnp
import numpy as np
from jax import lax

H = 64
LAT = 512
KD = 576
PREFIX = 384
CHILD_DEV = 96
PARENTS = 16
CHILDREN = 1536
CAP = 12
N_NODE = 16


def draw_child_query(key, part):
    key = jax.random.fold_in(key, 11)
    first = jax.random.fold_in(key, 0)
    values = jnp.clip(jax.random.normal(first, (CHILDREN, H, KD), jnp.float32), -4.0, 4.0)
    return values.astype(jnp.bfloat16)


def draw_parent_cache(key, part):
    key = jax.random.fold_in(key, 23)
    first = jax.random.fold_in(key, 0)
    values = jnp.clip(jax.random.normal(first, (PARENTS, PREFIX, KD), jnp.float32), -4.0, 4.0)
    return values.astype(jnp.bfloat16)


def draw_live_rows(key, part):
    key = jax.random.fold_in(key, 37)
    first, second = jax.random.split(key, 2)
    counts = jax.random.randint(first, (N_NODE,), 3 * CHILD_DEV // 4, CHILD_DEV + 1, jnp.int32)
    chosen = jax.random.randint(second, (), 0, N_NODE, jnp.int32)
    return jnp.where(jnp.arange(N_NODE, dtype=jnp.int32) == chosen, CHILD_DEV, counts).astype(jnp.int32)


def steps_of(own_key, dims, shards, low, top_value):
    level = 1.0
    for dim, shards_of in shards:
        draws = jax.random.uniform(jax.random.fold_in(jax.random.fold_in(own_key, 6), dim), (shards_of,), jnp.float32, low / len(shards), top_value / len(shards))
        level = level * jnp.repeat(jnp.exp(draws), dims[dim] // shards_of).reshape((-1,) + (1,) * (len(dims) - 1 - dim))
    return level


def assign_block(key, own, number, rows, number_of, top, bound, slope):
    order = jax.random.permutation(key, number_of)
    heavy_load, ordinary = shares(number_of, rows * top, bound, slope, True), shares(number_of, rows * top, bound, slope, False)
    places = jnp.arange(number_of)

    def named(sizes, rotation):
        used = int((sizes > 0).sum())
        fixed = max(1, used // 4)
        passed = fixed + (places - fixed + rotation * (used - fixed)) % max(1, number_of - fixed)
        return jnp.zeros((number_of,), jnp.int32).at[order[jnp.where(places < fixed, places, passed)]].set(jnp.asarray(sizes, jnp.int32))

    sizes = jnp.where(number % 4 == 0, named(heavy_load, number // 4), named(ordinary, number - number // 4 - 1))
    mixed = jax.random.permutation(jax.random.fold_in(own, 3), number_of)
    giver, sink = mixed[0:number_of // 2 * 2:2], mixed[1:number_of // 2 * 2:2]
    room = jnp.minimum(sizes[giver] - 1, bound - sizes[sink]) // 2
    room = jnp.where((giver == order[0]) | (sink == order[0]) | (sizes[sink] == 0), 0, jnp.maximum(room, 0))
    passed = jax.random.randint(jax.random.fold_in(own, 4), (number_of // 2,), 0, 1 << 20) % (room + 1)
    sizes = sizes.at[giver].add(-passed).at[sink].add(passed)
    members = jnp.searchsorted(jnp.cumsum(sizes), jnp.arange(rows * top), side="right").astype(jnp.int32)
    table = members.reshape(top, rows).T
    table = table[jax.random.permutation(jax.random.fold_in(own, 1), rows)]
    rotation = jax.random.randint(jax.random.fold_in(own, 2), (rows, 1), 0, top)
    return jnp.take_along_axis(table, (jnp.arange(top)[None, :] + rotation) % top, axis=1)


def shares(number_of, total, bound, skew, full):
    weights = [(1 << 20) // math.isqrt(standing ** skew) + 1 for standing in range(1, number_of + 1)]
    largest = bound if full else min(bound, max(-(-total // number_of), total * weights[0] // sum(weights)))
    least = 1 if total - largest >= number_of - 1 else 0
    given, surplus = [largest] + [least] * (number_of - 1), total - largest - least * (number_of - 1)
    while surplus > 0:
        movable = [i for i in range(1, number_of) if given[i] < largest] or [i for i in range(1, number_of) if given[i] < bound]
        pool, left = sum([weights[i] for i in movable]), surplus
        for i in movable:
            more = min(bound - given[i], max(1, left * weights[i] // pool), surplus)
            given[i] = given[i] + more
            surplus = surplus - more
    return np.array(given)


def bell_draw(rng, shape, width, reach, pieces=(), kind=jnp.bfloat16):
    values = width * jax.random.normal(rng, shape, jnp.float32)
    if pieces:
        values = values * steps_of(rng, shape, pieces, -0.22, 0.18)
    return jnp.clip(values, -reach, reach).astype(kind)


def setup_inputs(seed: int = 0, part: int = 0) -> dict:
    splits = jax.random.split(jax.random.key(seed), 7)
    own_keys = jax.random.split(jax.random.fold_in(splits[6], part), 7)
    child_query = draw_child_query(jax.random.fold_in(jax.random.fold_in(splits[6], part), 71), part)
    parent_cache = draw_parent_cache(jax.random.fold_in(jax.random.fold_in(splits[6], part), 71), part)
    child_latent = bell_draw(own_keys[2], (CHILDREN, KD), 1.0, 4.0, ((0, 16),))
    parent_place = jax.random.permutation(own_keys[3], PARENTS).astype(jnp.int32)
    child_parent_keys = jax.random.split(jax.random.fold_in(own_keys[4], 1), CHILDREN // CHILD_DEV)
    child_parent_turns = jax.random.permutation(jax.random.fold_in(own_keys[4], 3), CHILDREN // CHILD_DEV)
    child_parent = jax.vmap(lambda own, number: assign_block(jax.random.fold_in(own_keys[4], 2), own, number, CHILD_DEV, PARENTS, 1, CAP, 2))(child_parent_keys, child_parent_turns).reshape((CHILDREN, 1))
    live_rows = draw_live_rows(jax.random.fold_in(jax.random.fold_in(splits[6], part), 71), part)
    return {"child_query": child_query, "parent_cache": parent_cache, "child_latent": child_latent, "parent_place": parent_place, "child_parent": child_parent, "live_rows": live_rows}


SCALE = 0.07216878364870322


def softmax_parts(scores, own_score):
    highest = jnp.maximum(jnp.max(scores, axis=-1), own_score)
    expo = jnp.exp(scores - highest[..., None])
    own_expo = jnp.exp(own_score - highest)
    total = jnp.sum(expo, axis=-1) + own_expo
    return (expo / total[..., None]).astype(jnp.bfloat16), (own_expo / total).astype(jnp.bfloat16)


def reference(child_query, parent_cache, child_latent, parent_place, child_parent, live_rows):
    row_index = jnp.arange(CHILDREN, dtype=jnp.int32)
    device_of = row_index // CHILD_DEV
    live = (row_index % CHILD_DEV) < live_rows[device_of]
    stored_at = parent_place[child_parent[:, 0]].astype(jnp.int32)
    block_rows = math.gcd(CHILDREN, 64)
    block_count = CHILDREN // block_rows

    def one_block(inputs):
        query, latent, place = inputs
        cache = parent_cache[place].astype(jnp.float32)
        query32 = query.astype(jnp.float32)
        latent32 = latent.astype(jnp.float32)
        scores = jnp.einsum('bhk,bpk->bhp', query32, cache) * SCALE
        own_score = jnp.einsum('bhk,bk->bh', query32, latent32) * SCALE
        weights, own_weight = softmax_parts(scores, own_score)
        mixed = jnp.einsum('bhp,bpv->bhv', weights.astype(jnp.float32), cache[:, :, :LAT])
        mixed = mixed + own_weight.astype(jnp.float32)[..., None] * latent32[:, None, :LAT]
        return mixed.astype(jnp.bfloat16)

    result = lax.map(one_block, (child_query.reshape(block_count, block_rows, H, KD),
                                 child_latent.reshape(block_count, block_rows, KD),
                                 stored_at.reshape(block_count, block_rows)))
    result = result.reshape(CHILDREN, H, LAT)
    return jnp.where(live[:, None, None], result, jnp.zeros_like(result))
```

```python
import functools
import math

import jax
import jax.numpy as jnp
import numpy as np
from jax import lax
from jax.experimental import pallas as pl
from jax.experimental.pallas import tpu as pltpu
from jax.sharding import PartitionSpec as P

LAT = 512
SCALE = 0.07216878364870322
BLOCK = 4
ANY = pl.BlockSpec(memory_space=pl.ANY)
VMEM = pl.BlockSpec(memory_space=pltpu.VMEM)
SMEM = pl.BlockSpec(memory_space=pltpu.SMEM)


def sort_kernel(order, query, sorted_rows, sem):
    rows = query.shape[0]

    def fetch(j):
        return pltpu.make_async_copy(query.at[order[j]], sorted_rows.at[j], sem)

    @pl.loop(0, rows)
    def _(j):
        fetch(j).start()

    @pl.loop(0, rows)
    def _(j):
        fetch(j).wait()


def sort_rows(order, query):
    rows, heads, depth = query.shape
    return pl.pallas_call(
        sort_kernel,
        out_shape=pltpu.VMEM((rows + BLOCK, heads, depth), query.dtype),
        in_specs=[SMEM, ANY],
        out_specs=VMEM,
        scratch_shapes=[pltpu.SemaphoreType.DMA],
        compiler_params=pltpu.CompilerParams(vmem_limit_bytes=1024 * 1024),
        cost_estimate=pl.CostEstimate(flops=0, bytes_accessed=2 * query.size * 2, transcendentals=0),
    )(order, query)


def attend_kernel(first, arrays, aliased, order, starts, query, own, *refs):
    slots = refs[:arrays]
    refs = refs[arrays + (1 if aliased else 0):]
    out, kv, even, odd, ov, zeros, blocks, kv_sem, out_sem = refs
    count = arrays
    prefix = slots[0].shape[-1]
    width = kv.shape[2]
    rows = order.shape[0]
    heads = query.shape[1]
    size = BLOCK * heads
    dead = starts[starts.shape[0] - 1]
    base = starts[first]
    end = starts[first + count]

    def fetch_slot(s):
        return (
            pltpu.make_async_copy(slots[s], kv.at[s, :, pl.ds(0, prefix)], kv_sem.at[s, 0]),
            pltpu.make_async_copy(own, kv.at[s, :, pl.ds(prefix, width - prefix)], kv_sem.at[s, 1]),
        )

    for s in range(count):

        @pl.when(starts[first + s + 1] > starts[first + s])
        def _():
            for copy in fetch_slot(s):
                copy.start()

    if not aliased:
        zeros[...] = jnp.zeros_like(zeros)

        @pl.loop(dead, rows)
        def _(j):
            pltpu.make_async_copy(zeros, out.at[order[j]], out_sem).start()

    number = jnp.int32(0)
    for s in range(count):
        lo, hi = starts[first + s], starts[first + s + 1]
        more = (hi - lo + BLOCK - 1) // BLOCK

        def note(b, _):
            blocks[0, number + b] = s
            blocks[1, number + b] = lo + b * BLOCK
            blocks[2, number + b] = jnp.minimum(lo + (b + 1) * BLOCK, hi)
            return 0

        lax.fori_loop(0, more, note, 0)
        number = number + more
    for b in range(2):
        blocks[0, number + b] = 0
        blocks[1, number + b] = rows
        blocks[2, number + b] = rows

    for s in range(count):

        @pl.when(starts[first + s + 1] > starts[first + s])
        def _():
            for copy in fetch_slot(s):
                copy.wait()

    column = lax.broadcasted_iota(jnp.int32, (size, width), 1)
    row = lax.broadcasted_iota(jnp.int32, (size, width), 0) // heads
    offset = jnp.where(column < prefix, 0, column - prefix - row)

    def score(b, to):
        q = query[pl.ds(blocks[1, b], BLOCK)].reshape(size, query.shape[2])
        to[...] = jnp.dot(q, kv[blocks[0, b]], preferred_element_type=jnp.float32)

    def finish(b, scores):
        begin = blocks[1, b]
        seen = (column < prefix) | (offset == begin)
        s = jnp.where(seen, scores[...], -jnp.inf)
        top = jnp.max(s, axis=1, keepdims=True)
        expo = jnp.exp2((s - top) * (SCALE * math.log2(math.e)))
        total = jnp.sum(expo, axis=1, keepdims=True)
        weights = (expo * (1.0 / total)).astype(jnp.bfloat16)
        mixed = lax.dot_general(
            weights, kv[blocks[0, b], 0:LAT, :], (((1,), (1,)), ((), ())), preferred_element_type=jnp.float32
        )
        ov[pl.ds(begin, BLOCK)] = mixed.astype(jnp.bfloat16).reshape(BLOCK, heads, LAT)

    def send(b):
        @pl.loop(blocks[1, b], blocks[2, b])
        def _(j):
            pltpu.make_async_copy(ov.at[j], out.at[order[j]], out_sem).start()

    @pl.when(number > 0)
    def _():
        score(0, even)

        @pl.loop(0, (number + 1) // 2)
        def _(pair):
            b = pair * 2
            score(b + 1, odd)
            finish(b, even)
            score(b + 2, even)
            finish(b + 1, odd)
            send(b)
            send(b + 1)

    @pl.loop(base, end)
    def _(j):
        pltpu.make_async_copy(ov.at[j], out.at[order[j]], out_sem).wait()

    if not aliased:

        @pl.loop(dead, rows)
        def _(j):
            pltpu.make_async_copy(zeros, out.at[order[j]], out_sem).wait()


def attend(order, starts, first, query, own, slots, out=None):
    rows = order.shape[0]
    _, heads, depth = query.shape
    count = len(slots)
    prefix = slots[0].shape[-1]
    width = prefix + own.shape[1]
    aliased = out is not None
    operands = [order, starts, query, own, *slots] + ([out] if aliased else [])
    work = rows * heads * count // (starts.shape[0] - 1)
    return pl.pallas_call(
        functools.partial(attend_kernel, first, count, aliased),
        out_shape=jax.ShapeDtypeStruct((rows, heads, LAT), jnp.bfloat16),
        in_specs=[SMEM, SMEM, VMEM] + [ANY] * (len(operands) - 3),
        out_specs=ANY,
        scratch_shapes=[
            pltpu.VMEM((count, depth, width), jnp.bfloat16),
            pltpu.VMEM((BLOCK * heads, width), jnp.float32),
            pltpu.VMEM((BLOCK * heads, width), jnp.float32),
            pltpu.VMEM((rows + BLOCK, heads, LAT), jnp.bfloat16),
            pltpu.VMEM((heads, LAT), jnp.bfloat16),
            pltpu.SMEM((3, rows // BLOCK + count + 4), jnp.int32),
            pltpu.SemaphoreType.DMA((count, 2)),
            pltpu.SemaphoreType.DMA,
        ],
        input_output_aliases={len(operands) - 1: 0} if aliased else {},
        compiler_params=pltpu.CompilerParams(vmem_limit_bytes=20 * 1024 * 1024),
        cost_estimate=pl.CostEstimate(
            flops=2 * work * width * (depth + LAT),
            bytes_accessed=count * depth * width * 2 + work * LAT * 2,
            transcendentals=work * width,
        ),
    )(*operands)


def ring_of(nodes):
    chips = nodes // 2
    if chips == 8:
        return [0, 2, 4, 6, 7, 5, 3, 1]
    return list(range(chips))


def table(child_parent, parent_place, live_rows, ring, slot_of_distance, slot_count):
    rows = child_parent.shape[0]
    parents = parent_place.shape[0]
    chips = len(ring)
    me = lax.axis_index("node")
    core = me % 2
    position = np.zeros((parents,), np.int32)
    for at, chip in enumerate(ring):
        position[2 * chip] = position[2 * chip + 1] = at
    position = jnp.asarray(position)
    here = jnp.sum(jnp.where(jnp.arange(parents) == me, position, 0))
    ahead = jnp.where(core == 0, position - here, here - position)
    ahead = jnp.where(ahead < 0, ahead + chips, ahead)
    kind = 2 * ahead + jnp.where(jnp.arange(parents) % 2 == core, 0, 1)
    numbers = jnp.asarray(np.asarray(slot_of_distance, np.int32).reshape(-1))
    kinds = jnp.arange(parents, dtype=jnp.int32)
    slot_of_place = jnp.sum(jnp.where(kind[:, None] == kinds[None, :], numbers[None, :], 0), axis=1)
    slot_of_parent = jnp.sum(
        jnp.where(parent_place[:, None] == kinds[None, :], slot_of_place[None, :], 0), axis=1
    )
    named = child_parent == kinds[None, :]
    index = jnp.arange(rows, dtype=jnp.int32)
    slot = jnp.sum(jnp.where(named, slot_of_parent[None, :], 0), axis=1)
    slot = jnp.where(index < live_rows[0], slot, slot_count)
    key = slot * rows + index
    place = jnp.sum((key[None, :] < key[:, None]).astype(jnp.int32), axis=1)
    order = jnp.sum(jnp.where(place[:, None] == index[None, :], index[:, None], 0), axis=0)
    starts = jnp.sum(
        (slot[:, None] < jnp.arange(slot_count + 1, dtype=jnp.int32)[None, :]).astype(jnp.int32), axis=0
    )
    return order, starts, place


def shards(nodes, child_query, parent_cache, child_latent, parent_place, child_parent, live_rows):
    rows = child_query.shape[0]
    ring = ring_of(nodes)
    chips = len(ring)
    along = [(2 * ring[i], 2 * ring[(i + 1) % chips]) for i in range(chips)]
    along += [(2 * ring[(i + 1) % chips] + 1, 2 * ring[i] + 1) for i in range(chips)]
    across = [(i, i ^ 1) for i in range(nodes)]

    mine = jnp.swapaxes(parent_cache[0], 0, 1)
    other = lax.ppermute(mine, "node", across)
    phases = [[mine, other]]
    slot_of_distance = [[0, 1]] + [[0, 0] for _ in range(chips - 1)]
    number = 2
    streams = [mine, other]
    for k in range(1, chips // 2 + 1):
        both = 2 * k < chips
        streams = [lax.ppermute(a, "node", along) for a in streams[: 2 if both else 1]]
        for which, a in enumerate(streams):
            phases.append([a, lax.ppermute(a, "node", across)])
            if both:
                slot_of_distance[chips - k][which] = number
                slot_of_distance[k][1 - which] = number + 1
            else:
                slot_of_distance[k] = [number, number + 1]
            number += 2

    order, starts, place = table(child_parent, parent_place, live_rows, ring, slot_of_distance, number)
    padded = -(-rows // 128) * 128
    pick = (place[:, None] == jnp.arange(padded, dtype=jnp.int32)[None, :]).astype(jnp.bfloat16)
    own = lax.dot_general(
        child_latent, pick, (((0,), (0,)), ((), ())), preferred_element_type=jnp.float32
    ).astype(jnp.bfloat16)
    query = sort_rows(order, child_query)
    out, first = None, 0
    for slots in phases:
        out = attend(order, starts, first, query, own, slots, out)
        first += len(slots)
    return out


def solution(mesh):
    return jax.shard_map(
        functools.partial(shards, mesh.shape["node"]),
        mesh=mesh,
        in_specs=(
            P(("groups", "node"), None, None),
            P(("groups", "node"), None, None),
            P(("groups", "node"), None),
            P("groups"),
            P(("groups", "node"), None),
            P(("groups", "node")),
        ),
        out_specs=P(("groups", "node"), None, None),
        check_vma=False,
    )
```

```python
import functools
import math

import jax
import jax.numpy as jnp
import numpy as np
from jax import lax
from jax.experimental import pallas as pl
from jax.experimental.pallas import tpu as pltpu
from jax.sharding import PartitionSpec as P

LAT = 512
SCALE = 0.07216878364870322
BLOCK = 4
CHAINS = 3
COST = 4
ANY = pl.BlockSpec(memory_space=pl.ANY)
VMEM = pl.BlockSpec(memory_space=pltpu.VMEM)
SMEM = pl.BlockSpec(memory_space=pltpu.SMEM)


def prepare_kernel(me, numbers, position, place, parent, live, order, starts, slot_of):
    rows = parent.shape[0]
    parents = place.shape[0]
    slots = starts.shape[0] - 1
    chips = numbers.shape[0] // 2
    core = lax.rem(me[0], 2)
    here = position[me[0]]

    def name(p, _):
        at = place[p]
        ahead = jnp.where(core == 0, position[at] - here, here - position[at])
        ahead = jnp.where(ahead < 0, ahead + chips, ahead)
        slot_of[p] = numbers[2 * ahead + jnp.where(lax.rem(at, 2) == core, 0, 1)]
        return 0

    lax.fori_loop(0, parents, name, 0)

    def clear(s, _):
        starts[s] = 0
        return 0

    lax.fori_loop(0, slots + 1, clear, 0)

    def count(i, _):
        s = slot_of[parent[i]]
        starts[s] = starts[s] + 1
        return 0

    lax.fori_loop(0, live[0], count, 0)

    def ends(s, total):
        total = total + starts[s]
        starts[s] = total
        return total

    lax.fori_loop(0, slots, ends, jnp.int32(0))
    starts[slots] = live[0]

    def put(i, _):
        i = live[0] - 1 - i
        s = slot_of[parent[i]]
        j = starts[s] - 1
        starts[s] = j
        order[j] = i
        return 0

    lax.fori_loop(0, live[0], put, 0)

    def rest(i, _):
        order[i] = jnp.minimum(i, rows - 1)
        return 0

    lax.fori_loop(live[0], order.shape[0], rest, 0)


def prepare(me, numbers, position, place, parent, live):
    return pl.pallas_call(
        prepare_kernel,
        out_shape=(
            jax.ShapeDtypeStruct((parent.shape[0] + CHAINS * BLOCK,), jnp.int32),
            jax.ShapeDtypeStruct((numbers.shape[0] + 1,), jnp.int32),
        ),
        in_specs=[SMEM] * 6,
        out_specs=(SMEM, SMEM),
        scratch_shapes=[pltpu.SMEM((place.shape[0],), jnp.int32)],
        compiler_params=pltpu.CompilerParams(vmem_limit_bytes=1024 * 1024),
        cost_estimate=pl.CostEstimate(flops=0, bytes_accessed=8 * 1024 * 1024, transcendentals=0),
    )(me, numbers, position, place, parent, live)


def attend_kernel(first, arrays, aliased, order, starts, query, own, *refs):
    slots = refs[:arrays]
    refs = refs[arrays + (1 if aliased else 0):]
    out, sc, ow, ov, zeros, out_sem = refs
    rows, heads, depth = query.shape
    dead = starts[starts.shape[0] - 1]
    base = starts[first]
    end = starts[first + arrays]

    if not aliased:
        zeros[...] = jnp.zeros_like(zeros)

        @pl.loop(dead, rows)
        def _(j):
            pltpu.make_async_copy(zeros, out.at[order[j]], out_sem).start()

    def score(begin, cache, c):
        q = [query[order[begin + r]] for r in range(BLOCK)]
        sc[c] = jnp.dot(jnp.concatenate(q), cache[...], preferred_element_type=jnp.float32)
        for r in range(BLOCK):
            mine = jnp.sum(q[r].astype(jnp.float32) * own[order[begin + r]], axis=1, keepdims=True)
            ow[c, r * heads:(r + 1) * heads] = jnp.broadcast_to(mine, (heads, ow.shape[2]))

    def finish(begin, cache, c):
        s = sc[c]
        mine = ow[c][:, 0:1]
        top = jnp.maximum(jnp.max(s, axis=1, keepdims=True), mine)
        expo = jnp.exp2((s - top) * (SCALE * math.log2(math.e)))
        mine = jnp.exp2((mine - top) * (SCALE * math.log2(math.e)))
        share = 1.0 / (jnp.sum(expo, axis=1, keepdims=True) + mine)
        weights = (expo * share).astype(jnp.bfloat16)
        mine = (mine * share).astype(jnp.bfloat16).astype(jnp.float32)
        mixed = lax.dot_general(
            weights, cache[0:LAT, :], (((1,), (1,)), ((), ())), preferred_element_type=jnp.float32
        )
        for r in range(BLOCK):
            part = slice(r * heads, (r + 1) * heads)
            total = mixed[part] + mine[part] * own[order[begin + r]][:, 0:LAT]
            ov[begin + r] = total.astype(jnp.bfloat16)

    def work(begin, cache, blocks):
        for c in range(blocks):
            score(begin + c * BLOCK, cache, c)
        for c in range(blocks):
            finish(begin + c * BLOCK, cache, c)

    for s in range(arrays):
        lo, hi = starts[first + s], starts[first + s + 1]

        @pl.loop(0, (hi - lo + CHAINS * BLOCK - 1) // (CHAINS * BLOCK))
        def _(part):
            begin = lo + part * (CHAINS * BLOCK)
            stop = jnp.minimum(begin + CHAINS * BLOCK, hi)
            need = (stop - begin + BLOCK - 1) // BLOCK
            for blocks in range(1, CHAINS + 1):

                @pl.when(need == blocks)
                def _():
                    work(begin, slots[s], blocks)

            @pl.loop(begin, stop)
            def _(j):
                pltpu.make_async_copy(ov.at[j], out.at[order[j]], out_sem).start()

    @pl.loop(base, end)
    def _(j):
        pltpu.make_async_copy(ov.at[0], out.at[0], out_sem).wait()

    if not aliased:

        @pl.loop(dead, rows)
        def _(j):
            pltpu.make_async_copy(zeros, out.at[0], out_sem).wait()


def attend(order, starts, first, query, own, slots, out=None):
    rows, heads, depth = query.shape
    prefix = slots[0].shape[-1]
    aliased = out is not None
    operands = [order, starts, query, own, *slots] + ([out] if aliased else [])
    work = rows * heads * len(slots) // (starts.shape[0] - 1)
    return pl.pallas_call(
        functools.partial(attend_kernel, first, len(slots), aliased),
        out_shape=jax.ShapeDtypeStruct((rows, heads, LAT), jnp.bfloat16),
        in_specs=[SMEM, SMEM, VMEM, VMEM] + [VMEM] * len(slots) + [ANY] * aliased,
        out_specs=ANY,
        scratch_shapes=[
            pltpu.VMEM((CHAINS, BLOCK * heads, prefix), jnp.float32),
            pltpu.VMEM((CHAINS, BLOCK * heads, 128), jnp.float32),
            pltpu.VMEM((rows + CHAINS * BLOCK, heads, LAT), jnp.bfloat16),
            pltpu.VMEM((heads, LAT), jnp.bfloat16),
            pltpu.SemaphoreType.DMA,
        ],
        input_output_aliases={len(operands) - 1: 0} if aliased else {},
        compiler_params=pltpu.CompilerParams(vmem_limit_bytes=20 * 1024 * 1024),
        cost_estimate=pl.CostEstimate(
            flops=COST * 2 * work * prefix * (depth + LAT),
            bytes_accessed=COST * (len(slots) * depth * prefix * 2 + work * LAT * 2),
            transcendentals=COST * work * prefix,
        ),
    )(*operands)


def ring_of(nodes):
    chips = nodes // 2
    if chips == 8:
        return [0, 2, 4, 6, 7, 5, 3, 1]
    return list(range(chips))


def shards(nodes, child_query, parent_cache, child_latent, parent_place, child_parent, live_rows):
    ring = ring_of(nodes)
    chips = len(ring)
    along = [(2 * ring[i], 2 * ring[(i + 1) % chips]) for i in range(chips)]
    along += [(2 * ring[(i + 1) % chips] + 1, 2 * ring[i] + 1) for i in range(chips)]
    across = [(i, i ^ 1) for i in range(nodes)]

    mine = jnp.swapaxes(parent_cache[0], 0, 1)
    other = lax.ppermute(mine, "node", across)
    phases = [[mine, other]]
    slot_of_distance = [[0, 1]] + [[0, 0] for _ in range(chips - 1)]
    number = 2
    streams = [mine, other]
    for k in range(1, chips // 2 + 1):
        both = 2 * k < chips
        streams = [lax.ppermute(a, "node", along) for a in streams[: 2 if both else 1]]
        for which, a in enumerate(streams):
            phases.append([a, lax.ppermute(a, "node", across)])
            if both:
                slot_of_distance[chips - k][which] = number
                slot_of_distance[k][1 - which] = number + 1
            else:
                slot_of_distance[k] = [number, number + 1]
            number += 2

    position = np.zeros((nodes,), np.int32)
    for at, chip in enumerate(ring):
        position[2 * chip:2 * chip + 2] = at
    order, starts = prepare(
        jnp.reshape(lax.axis_index("node"), (1,)),
        jnp.asarray(np.asarray(slot_of_distance, np.int32).reshape(-1)),
        jnp.asarray(position),
        parent_place,
        child_parent[:, 0],
        live_rows,
    )
    own = child_latent.astype(jnp.float32)[:, None, :]
    out, first = None, 0
    for slots in phases:
        out = attend(order, starts, first, child_query, own, slots, out)
        first += len(slots)
    return out


def solution(mesh):
    return jax.shard_map(
        functools.partial(shards, mesh.shape["node"]),
        mesh=mesh,
        in_specs=(
            P(("groups", "node"), None, None),
            P(("groups", "node"), None, None),
            P(("groups", "node"), None),
            P("groups"),
            P(("groups", "node"), None),
            P(("groups", "node")),
        ),
        out_specs=P(("groups", "node"), None, None),
        check_vma=False,
    )
```

```python
import functools
import math

import jax
import jax.numpy as jnp
from jax import lax
from jax.experimental import pallas as pl
from jax.experimental.pallas import tpu as pltpu
from jax.sharding import PartitionSpec as P

LAT = 512
SCALE = 0.07216878364870322
BLOCK = 4
COST = 4
ANY = pl.BlockSpec(memory_space=pl.ANY)
VMEM = pl.BlockSpec(memory_space=pltpu.VMEM)
SMEM = pl.BlockSpec(memory_space=pltpu.SMEM)


def position_of(chip, chips):
    if chips == 8:
        return jnp.where(chip % 2 == 0, chip // 2, 7 - chip // 2)
    return chip


def slot_of(ahead, same, chips):
    far = jnp.minimum(ahead, chips - ahead)
    slot = 4 * far - 2 + jnp.where(2 * ahead > chips, jnp.where(same, 0, 2), jnp.where(same, 3, 1))
    slot = jnp.where(2 * ahead == chips, 4 * far - 2 + jnp.where(same, 0, 1), slot)
    return jnp.where(ahead == 0, jnp.where(same, 0, 1), slot)


def prepare_kernel(place_in, parent_in, live_in, query_in, mine_in, order, starts, query, mine, place, parent, live, slots, sem):
    rows = parent.shape[1]
    parents = place.shape[0]
    count = starts.shape[0] - 1
    chips = parents // 2
    big = [
        pltpu.make_async_copy(query_in, query, sem.at[0]),
        pltpu.make_async_copy(mine_in, mine, sem.at[1]),
    ]
    small = [
        pltpu.make_async_copy(place_in, place, sem.at[2]),
        pltpu.make_async_copy(parent_in, parent, sem.at[3]),
        pltpu.make_async_copy(live_in, live, sem.at[4]),
    ]
    for copy in small + big:
        copy.start()
    for copy in small:
        copy.wait()
    me = lax.axis_index("node")
    core = me % 2
    here = position_of(me // 2, chips)

    def name(p, _):
        at = place[p]
        there = position_of(at // 2, chips)
        ahead = jnp.where(core == 0, there - here, here - there)
        ahead = jnp.where(ahead < 0, ahead + chips, ahead)
        slots[p] = slot_of(ahead, at % 2 == core, chips)
        return 0

    lax.fori_loop(0, parents, name, 0)

    def clear(s, _):
        starts[s] = 0
        return 0

    lax.fori_loop(0, count + 1, clear, 0)

    def tally(i, _):
        s = slots[parent[0, i]]
        starts[s] = starts[s] + 1
        return 0

    lax.fori_loop(0, live[0], tally, 0)

    def ends(s, total):
        total = total + starts[s]
        starts[s] = total
        return total

    lax.fori_loop(0, count, ends, jnp.int32(0))
    starts[count] = live[0]

    def put(i, _):
        i = live[0] - 1 - i
        s = slots[parent[0, i]]
        j = starts[s] - 1
        starts[s] = j
        order[j] = i
        return 0

    lax.fori_loop(0, live[0], put, 0)

    def rest(i, _):
        order[i] = jnp.minimum(i, rows - 1)
        return 0

    lax.fori_loop(live[0], order.shape[0], rest, 0)
    for copy in big:
        copy.wait()


def prepare(place, parent, live, query, mine):
    rows, parents = parent.shape[1], place.shape[0]
    return pl.pallas_call(
        prepare_kernel,
        out_shape=(
            jax.ShapeDtypeStruct((rows + 2 * BLOCK,), jnp.int32),
            jax.ShapeDtypeStruct((parents + 1,), jnp.int32),
            pltpu.VMEM(query.shape, query.dtype),
            pltpu.VMEM(mine.shape, mine.dtype),
        ),
        in_specs=[ANY] * 5,
        out_specs=(SMEM, SMEM, VMEM, VMEM),
        scratch_shapes=[
            pltpu.SMEM(place.shape, jnp.int32),
            pltpu.SMEM(parent.shape, jnp.int32),
            pltpu.SMEM(live.shape, jnp.int32),
            pltpu.SMEM(place.shape, jnp.int32),
            pltpu.SemaphoreType.DMA((5,)),
        ],
        compiler_params=pltpu.CompilerParams(vmem_limit_bytes=46 * 1024 * 1024),
        cost_estimate=pl.CostEstimate(flops=0, bytes_accessed=2 * query.size * 2, transcendentals=0),
    )(place, parent, live, query, mine)


def attend_kernel(first, arrays, aliased, order, starts, query, own, *refs):
    slots = refs[:arrays]
    refs = refs[arrays + (1 if aliased else 0):]
    out, kv, even, odd, ov, zeros, blocks, out_sem = refs
    rows, heads, depth = query.shape
    prefix = slots[0].shape[-1]
    width = kv.shape[2]
    dead = starts[starts.shape[0] - 1]
    base = starts[first]
    end = starts[first + arrays]

    if not aliased:
        zeros[...] = jnp.zeros_like(zeros)

        @pl.loop(dead, rows)
        def _(j):
            pltpu.make_async_copy(zeros, out.at[order[j]], out_sem).start()

    number = jnp.int32(0)
    for s in range(arrays):
        kv[s, :, 0:prefix] = slots[s][...]
        kv[s, :, prefix:width] = own[...]
        lo, hi = starts[first + s], starts[first + s + 1]
        more = (hi - lo + BLOCK - 1) // BLOCK

        def note(b, _):
            blocks[0, number + b] = s
            blocks[1, number + b] = lo + b * BLOCK
            blocks[2, number + b] = jnp.minimum(lo + (b + 1) * BLOCK, hi)
            return 0

        lax.fori_loop(0, more, note, 0)
        number = number + more
    for b in range(2):
        blocks[0, number + b] = 0
        blocks[1, number + b] = rows
        blocks[2, number + b] = rows

    column = lax.broadcasted_iota(jnp.int32, (heads, width - prefix), 1)

    def score(b, to):
        begin = blocks[1, b]
        q = jnp.concatenate([query[order[begin + r]] for r in range(BLOCK)])
        to[...] = jnp.dot(q, kv[blocks[0, b]], preferred_element_type=jnp.float32)

    def finish(b, scores):
        begin = blocks[1, b]
        mine = [
            jnp.where(column == order[begin + r], scores[r * heads:(r + 1) * heads, prefix:width], -jnp.inf)
            for r in range(BLOCK)
        ]
        s = jnp.concatenate([scores[:, 0:prefix], jnp.concatenate(mine)], axis=1)
        top = jnp.max(s, axis=1, keepdims=True)
        expo = jnp.exp2((s - top) * (SCALE * math.log2(math.e)))
        total = jnp.sum(expo, axis=1, keepdims=True)
        weights = (expo * (1.0 / total)).astype(jnp.bfloat16)
        mixed = lax.dot_general(
            weights, kv[blocks[0, b], 0:LAT, :], (((1,), (1,)), ((), ())), preferred_element_type=jnp.float32
        )
        ov[pl.ds(begin, BLOCK)] = mixed.astype(jnp.bfloat16).reshape(BLOCK, heads, LAT)

    def send(b):
        @pl.loop(blocks[1, b], blocks[2, b])
        def _(j):
            pltpu.make_async_copy(ov.at[j], out.at[order[j]], out_sem).start()

    @pl.when(number > 0)
    def _():
        score(0, even)

        @pl.loop(0, (number + 1) // 2)
        def _(pair):
            b = pair * 2
            score(b + 1, odd)
            finish(b, even)
            score(b + 2, even)
            finish(b + 1, odd)
            send(b)
            send(b + 1)

    @pl.loop(base, end)
    def _(j):
        pltpu.make_async_copy(ov.at[0], out.at[0], out_sem).wait()

    if not aliased:

        @pl.loop(dead, rows)
        def _(j):
            pltpu.make_async_copy(zeros, out.at[0], out_sem).wait()


def attend(order, starts, first, query, own, slots, out=None):
    rows, heads, depth = query.shape
    count = len(slots)
    prefix = slots[0].shape[-1]
    width = prefix + own.shape[1]
    aliased = out is not None
    operands = [order, starts, query, own, *slots] + ([out] if aliased else [])
    work = rows * heads * count // (starts.shape[0] - 1)
    return pl.pallas_call(
        functools.partial(attend_kernel, first, count, aliased),
        out_shape=jax.ShapeDtypeStruct((rows, heads, LAT), jnp.bfloat16),
        in_specs=[SMEM, SMEM, VMEM, VMEM] + [VMEM] * count + [ANY] * aliased,
        out_specs=ANY,
        scratch_shapes=[
            pltpu.VMEM((count, depth, width), jnp.bfloat16),
            pltpu.VMEM((BLOCK * heads, width), jnp.float32),
            pltpu.VMEM((BLOCK * heads, width), jnp.float32),
            pltpu.VMEM((rows + BLOCK, heads, LAT), jnp.bfloat16),
            pltpu.VMEM((heads, LAT), jnp.bfloat16),
            pltpu.SMEM((3, rows // BLOCK + count + 4), jnp.int32),
            pltpu.SemaphoreType.DMA,
        ],
        input_output_aliases={len(operands) - 1: 0} if aliased else {},
        compiler_params=pltpu.CompilerParams(vmem_limit_bytes=20 * 1024 * 1024),
        cost_estimate=pl.CostEstimate(
            flops=COST * 2 * work * width * (depth + LAT),
            bytes_accessed=COST * (count * depth * width * 2 + work * LAT * 2),
            transcendentals=COST * work * width,
        ),
    )(*operands)


def ring_of(nodes):
    chips = nodes // 2
    if chips == 8:
        return [0, 2, 4, 6, 7, 5, 3, 1]
    return list(range(chips))


def shards(nodes, child_query, parent_cache, child_latent, parent_place, child_parent, live_rows):
    rows = child_query.shape[0]
    ring = ring_of(nodes)
    chips = len(ring)
    along = [(2 * ring[i], 2 * ring[(i + 1) % chips]) for i in range(chips)]
    along += [(2 * ring[(i + 1) % chips] + 1, 2 * ring[i] + 1) for i in range(chips)]
    across = [(i, i ^ 1) for i in range(nodes)]

    mine = jnp.swapaxes(parent_cache[0], 0, 1)
    other = lax.ppermute(mine, "node", across)
    order, starts, query, kept = prepare(
        parent_place, jnp.swapaxes(child_parent, 0, 1), live_rows, child_query, mine
    )
    padded = -(-rows // 128) * 128
    pick = jnp.arange(rows)[:, None] == jnp.arange(padded)[None, :]
    own = lax.dot_general(
        child_latent, pick.astype(jnp.bfloat16), (((0,), (0,)), ((), ())), preferred_element_type=jnp.float32
    ).astype(jnp.bfloat16)

    out = attend(order, starts, 0, query, own, [kept, other])
    streams = [mine, other]
    first = 2
    for k in range(1, chips // 2 + 1):
        streams = [lax.ppermute(a, "node", along) for a in streams[: 2 if 2 * k < chips else 1]]
        for a in streams:
            out = attend(order, starts, first, query, own, [a, lax.ppermute(a, "node", across)], out)
            first += 2
    return out


def solution(mesh):
    return jax.shard_map(
        functools.partial(shards, mesh.shape["node"]),
        mesh=mesh,
        in_specs=(
            P(("groups", "node"), None, None),
            P(("groups", "node"), None, None),
            P(("groups", "node"), None),
            P("groups"),
            P(("groups", "node"), None),
            P(("groups", "node")),
        ),
        out_specs=P(("groups", "node"), None, None),
        check_vma=False,
    )
```

```python
import functools
import math

import jax
import jax.numpy as jnp
from jax import lax
from jax.experimental import pallas as pl
from jax.experimental.pallas import tpu as pltpu
from jax.sharding import PartitionSpec as P

LAT = 512
SCALE = 0.07216878364870322
BLOCK = 6
COST = 4
ANY = pl.BlockSpec(memory_space=pl.ANY)
VMEM = pl.BlockSpec(memory_space=pltpu.VMEM)
SMEM = pl.BlockSpec(memory_space=pltpu.SMEM)


def position_of(chip, chips):
    if chips == 8:
        return jnp.where(chip % 2 == 0, chip // 2, 7 - chip // 2)
    return chip


def slot_of(ahead, same, chips):
    far = jnp.minimum(ahead, chips - ahead)
    slot = 4 * far - 2 + jnp.where(2 * ahead > chips, jnp.where(same, 0, 2), jnp.where(same, 3, 1))
    slot = jnp.where(2 * ahead == chips, 4 * far - 2 + jnp.where(same, 0, 1), slot)
    return jnp.where(ahead == 0, jnp.where(same, 0, 1), slot)


def prepare_kernel(
    place_in, parent_in, live_in, query_in, mine_in, _, order, starts, query, mine, __, place, parent, live, slots, names, sem
):
    rows = parent.shape[1]
    parents = place.shape[0]
    dead = starts.shape[0] - 1
    chips = parents // 2
    big = [
        pltpu.make_async_copy(query_in, query, sem.at[0]),
        pltpu.make_async_copy(mine_in, mine, sem.at[1]),
    ]
    small = [
        pltpu.make_async_copy(place_in, place, sem.at[2]),
        pltpu.make_async_copy(parent_in, parent, sem.at[3]),
        pltpu.make_async_copy(live_in, live, sem.at[4]),
    ]
    for copy in small + big:
        copy.start()
    for copy in small:
        copy.wait()
    me = lax.axis_index("node")
    core = me % 2
    here = position_of(me // 2, chips)
    alive = live[0]

    def name(p, _):
        at = place[p]
        there = position_of(at // 2, chips)
        ahead = jnp.where(core == 0, there - here, here - there)
        ahead = jnp.where(ahead < 0, ahead + chips, ahead)
        names[p] = slot_of(ahead, at % 2 == core, chips)
        starts[p] = 0
        return 0

    lax.fori_loop(0, parents, name, 0, unroll=4)
    starts[dead] = 0

    def tally(i, _):
        s = jnp.where(i < alive, names[parent[0, i]], dead)
        slots[i] = s
        starts[s] = starts[s] + 1
        return 0

    lax.fori_loop(0, rows, tally, 0, unroll=8)

    def ends(s, total):
        total = total + starts[s]
        starts[s] = total
        return total

    lax.fori_loop(0, dead + 1, ends, jnp.int32(0))

    def put(i, _):
        i = rows - 1 - i
        s = slots[i]
        j = starts[s] - 1
        starts[s] = j
        order[j] = i
        return 0

    lax.fori_loop(0, rows, put, 0, unroll=8)
    for i in range(rows, order.shape[0]):
        order[i] = 0
    for copy in big:
        copy.wait()


def prepare(place, parent, live, query, mine, other):
    rows, parents = parent.shape[1], place.shape[0]
    return pl.pallas_call(
        prepare_kernel,
        out_shape=(
            jax.ShapeDtypeStruct((rows + 2 * BLOCK,), jnp.int32),
            jax.ShapeDtypeStruct((parents + 1,), jnp.int32),
            pltpu.VMEM(query.shape, query.dtype),
            pltpu.VMEM(mine.shape, mine.dtype),
            pltpu.VMEM(other.shape, other.dtype),
        ),
        in_specs=[ANY] * 5 + [VMEM],
        out_specs=(SMEM, SMEM, VMEM, VMEM, VMEM),
        scratch_shapes=[
            pltpu.SMEM(place.shape, jnp.int32),
            pltpu.SMEM(parent.shape, jnp.int32),
            pltpu.SMEM(live.shape, jnp.int32),
            pltpu.SMEM((rows,), jnp.int32),
            pltpu.SMEM(place.shape, jnp.int32),
            pltpu.SemaphoreType.DMA((5,)),
        ],
        input_output_aliases={5: 4},
        compiler_params=pltpu.CompilerParams(vmem_limit_bytes=46 * 1024 * 1024),
        cost_estimate=pl.CostEstimate(flops=0, bytes_accessed=2 * query.size * 2, transcendentals=0),
    )(place, parent, live, query, mine, other)


def attend_kernel(first, before, last, arrays, order, starts, query, own, *refs):
    slots = refs[:arrays]
    out, ov, kv, even, odd, zeros, blocks, out_sem = refs[-8:]
    done = refs[arrays] if before else None
    rows, heads, depth = query.shape
    prefix = slots[0].shape[-1]
    width = kv.shape[2]
    base = starts[first]
    end = starts[first + arrays]

    if before:
        from_row, to_row = starts[first - before], base
    else:
        zeros[...] = jnp.zeros_like(zeros)
        from_row, to_row = starts[starts.shape[0] - 1], rows

    @pl.loop(from_row, to_row)
    def _(j):
        pltpu.make_async_copy(done.at[j] if before else zeros, out.at[order[j]], out_sem).start()

    number = jnp.int32(0)
    for s in range(arrays):
        kv[s, :, 0:prefix] = slots[s][...]
        kv[s, :, prefix:width] = own[...]
        lo, hi = starts[first + s], starts[first + s + 1]
        more = (hi - lo + BLOCK - 1) // BLOCK

        def note(b, _):
            blocks[0, number + b] = s
            blocks[1, number + b] = lo + b * BLOCK
            blocks[2, number + b] = jnp.minimum(lo + (b + 1) * BLOCK, hi)
            return 0

        lax.fori_loop(0, more, note, 0)
        number = number + more
    for b in range(2):
        blocks[0, number + b] = 0
        blocks[1, number + b] = rows
        blocks[2, number + b] = rows

    column = lax.broadcasted_iota(jnp.int32, (heads, width - prefix), 1)

    def score(b, to):
        begin = blocks[1, b]
        q = jnp.concatenate([query[order[begin + r]] for r in range(BLOCK)])
        to[...] = jnp.dot(q, kv[blocks[0, b]], preferred_element_type=jnp.float32)

    def finish(b, scores):
        begin = blocks[1, b]
        mine = [
            jnp.where(column == order[begin + r], scores[r * heads:(r + 1) * heads, prefix:width], -jnp.inf)
            for r in range(BLOCK)
        ]
        s = jnp.concatenate([scores[:, 0:prefix], jnp.concatenate(mine)], axis=1)
        top = jnp.max(s, axis=1, keepdims=True)
        expo = jnp.exp2((s - top) * (SCALE * math.log2(math.e)))
        total = jnp.sum(expo, axis=1, keepdims=True)
        weights = (expo * (1.0 / total)).astype(jnp.bfloat16)
        mixed = lax.dot_general(
            weights, kv[blocks[0, b], 0:LAT, :], (((1,), (1,)), ((), ())), preferred_element_type=jnp.float32
        )
        ov[pl.ds(begin, BLOCK)] = mixed.astype(jnp.bfloat16).reshape(BLOCK, heads, LAT)

    def send(b):
        @pl.loop(blocks[1, b], blocks[2, b])
        def _(j):
            pltpu.make_async_copy(ov.at[j], out.at[order[j]], out_sem).start()

    @pl.when(number > 0)
    def _():
        @pl.loop(0, (number + 1) // 2)
        def _(pair):
            b = pair * 2
            score(b, even)
            score(b + 1, odd)
            finish(b, even)
            finish(b + 1, odd)
            if last:
                send(b)
                send(b + 1)

    @pl.loop(from_row, to_row)
    def _(j):
        pltpu.make_async_copy(zeros, out.at[0], out_sem).wait()

    if last:

        @pl.loop(base, end)
        def _(j):
            pltpu.make_async_copy(zeros, out.at[0], out_sem).wait()


def attend(order, starts, first, query, own, slots, before=0, done=None, out=None, last=False):
    rows, heads, depth = query.shape
    count = len(slots)
    prefix = slots[0].shape[-1]
    width = prefix + own.shape[1]
    operands = [order, starts, query, own, *slots] + ([done, out] if before else [])
    work = rows * heads * count // (starts.shape[0] - 1)
    result = jax.ShapeDtypeStruct((rows, heads, LAT), jnp.bfloat16)
    made = pltpu.VMEM((rows + BLOCK, heads, LAT), jnp.bfloat16)
    return pl.pallas_call(
        functools.partial(attend_kernel, first, before, last, count),
        out_shape=result if last else (result, made),
        in_specs=[SMEM, SMEM, VMEM, VMEM] + [VMEM] * count + [VMEM, ANY] * (before > 0),
        out_specs=ANY if last else (ANY, VMEM),
        scratch_shapes=[made] * last + [
            pltpu.VMEM((count, depth, width), jnp.bfloat16),
            pltpu.VMEM((BLOCK * heads, width), jnp.float32),
            pltpu.VMEM((BLOCK * heads, width), jnp.float32),
            pltpu.VMEM((heads, LAT), jnp.bfloat16),
            pltpu.SMEM((3, rows // BLOCK + count + 4), jnp.int32),
            pltpu.SemaphoreType.DMA,
        ],
        input_output_aliases={len(operands) - 1: 0} if before else {},
        compiler_params=pltpu.CompilerParams(vmem_limit_bytes=16 * 1024 * 1024),
        cost_estimate=pl.CostEstimate(
            flops=COST * 2 * work * width * (depth + LAT),
            bytes_accessed=COST * (count * depth * width * 2 + work * LAT * 2),
            transcendentals=COST * work * width,
        ),
    )(*operands)


def ring_of(nodes):
    chips = nodes // 2
    if chips == 8:
        return [0, 2, 4, 6, 7, 5, 3, 1]
    return list(range(chips))


def shards(nodes, child_query, parent_cache, child_latent, parent_place, child_parent, live_rows):
    rows = child_query.shape[0]
    ring = ring_of(nodes)
    chips = len(ring)
    along = [(2 * ring[i], 2 * ring[(i + 1) % chips]) for i in range(chips)]
    along += [(2 * ring[(i + 1) % chips] + 1, 2 * ring[i] + 1) for i in range(chips)]
    across = [(i, i ^ 1) for i in range(nodes)]

    mine = jnp.swapaxes(parent_cache[0], 0, 1)
    other = lax.ppermute(mine, "node", across)
    order, starts, query, kept, other = prepare(
        parent_place, jnp.swapaxes(child_parent, 0, 1), live_rows, child_query, mine, other
    )
    padded = -(-rows // 128) * 128
    pick = jnp.arange(rows)[:, None] == jnp.arange(padded)[None, :]
    own = lax.dot_general(
        child_latent, pick.astype(jnp.bfloat16), (((0,), (0,)), ((), ())), preferred_element_type=jnp.float32
    ).astype(jnp.bfloat16)

    phases = [[kept, other]]
    streams = [mine, other]
    for k in range(1, chips // 2 + 1):
        streams = [lax.ppermute(a, "node", along) for a in streams[: 2 if 2 * k < chips else 1]]
        phases += [[a, lax.ppermute(a, "node", across)] for a in streams]
    first, before, result = 0, 0, (None, None)
    for slots in phases:
        last = slots is phases[-1]
        result = attend(order, starts, first, query, own, slots, before, result[1], result[0], last)
        first, before = first + len(slots), len(slots)
    return result


def solution(mesh):
    return jax.shard_map(
        functools.partial(shards, mesh.shape["node"]),
        mesh=mesh,
        in_specs=(
            P(("groups", "node"), None, None),
            P(("groups", "node"), None, None),
            P(("groups", "node"), None),
            P("groups"),
            P(("groups", "node"), None),
            P(("groups", "node")),
        ),
        out_specs=P(("groups", "node"), None, None),
        check_vma=False,
    )
```

```python
import functools
import math

import jax
import jax.numpy as jnp
from jax import lax
from jax.experimental import pallas as pl
from jax.experimental.pallas import tpu as pltpu
from jax.sharding import PartitionSpec as P

LAT = 512
SCALE = 0.07216878364870322
BLOCK = 6
COST = 4
ANY = pl.BlockSpec(memory_space=pl.ANY)
VMEM = pl.BlockSpec(memory_space=pltpu.VMEM)
SMEM = pl.BlockSpec(memory_space=pltpu.SMEM)


def position_of(chip, chips):
    if chips == 8:
        return jnp.where(chip % 2 == 0, chip // 2, 7 - chip // 2)
    return chip


def slot_of(ahead, same, chips):
    far = jnp.minimum(ahead, chips - ahead)
    slot = 4 * far - 2 + jnp.where(2 * ahead > chips, jnp.where(same, 0, 2), jnp.where(same, 3, 1))
    slot = jnp.where(2 * ahead == chips, 4 * far - 2 + jnp.where(same, 0, 1), slot)
    return jnp.where(ahead == 0, jnp.where(same, 0, 1), slot)


def prepare_kernel(
    place_in, parent_in, live_in, query_in, mine_in, _, order, starts, query, mine, __, place, parent, live, slots, names, sem
):
    rows = parent.shape[1]
    parents = place.shape[0]
    dead = starts.shape[0] - 1
    chips = parents // 2
    big = [
        pltpu.make_async_copy(query_in, query, sem.at[0]),
        pltpu.make_async_copy(mine_in, mine, sem.at[1]),
    ]
    small = [
        pltpu.make_async_copy(place_in, place, sem.at[2]),
        pltpu.make_async_copy(parent_in, parent, sem.at[3]),
        pltpu.make_async_copy(live_in, live, sem.at[4]),
    ]
    for copy in small + big:
        copy.start()
    for copy in small:
        copy.wait()
    me = lax.axis_index("node")
    core = me % 2
    here = position_of(me // 2, chips)
    alive = live[0]

    def name(p, _):
        at = place[p]
        there = position_of(at // 2, chips)
        ahead = jnp.where(core == 0, there - here, here - there)
        ahead = jnp.where(ahead < 0, ahead + chips, ahead)
        names[p] = slot_of(ahead, at % 2 == core, chips)
        starts[p] = 0
        return 0

    lax.fori_loop(0, parents, name, 0, unroll=4)
    starts[dead] = 0

    def tally(i, _):
        s = jnp.where(i < alive, names[parent[0, i]], dead)
        slots[i] = s
        starts[s] = starts[s] + 1
        return 0

    lax.fori_loop(0, rows, tally, 0, unroll=8)

    def ends(s, total):
        total = total + starts[s]
        starts[s] = total
        return total

    lax.fori_loop(0, dead + 1, ends, jnp.int32(0))

    def put(i, _):
        i = rows - 1 - i
        s = slots[i]
        j = starts[s] - 1
        starts[s] = j
        order[j] = i
        return 0

    lax.fori_loop(0, rows, put, 0, unroll=8)
    for i in range(rows, order.shape[0]):
        order[i] = 0
    for copy in big:
        copy.wait()


def prepare(place, parent, live, query, mine, other):
    rows, parents = parent.shape[1], place.shape[0]
    return pl.pallas_call(
        prepare_kernel,
        out_shape=(
            jax.ShapeDtypeStruct((rows + 2 * BLOCK,), jnp.int32),
            jax.ShapeDtypeStruct((parents + 1,), jnp.int32),
            pltpu.VMEM(query.shape, query.dtype),
            pltpu.VMEM(mine.shape, mine.dtype),
            pltpu.VMEM(other.shape, other.dtype),
        ),
        in_specs=[ANY] * 5 + [VMEM],
        out_specs=(SMEM, SMEM, VMEM, VMEM, VMEM),
        scratch_shapes=[
            pltpu.SMEM(place.shape, jnp.int32),
            pltpu.SMEM(parent.shape, jnp.int32),
            pltpu.SMEM(live.shape, jnp.int32),
            pltpu.SMEM((rows,), jnp.int32),
            pltpu.SMEM(place.shape, jnp.int32),
            pltpu.SemaphoreType.DMA((5,)),
        ],
        input_output_aliases={5: 4},
        compiler_params=pltpu.CompilerParams(vmem_limit_bytes=46 * 1024 * 1024),
        cost_estimate=pl.CostEstimate(flops=0, bytes_accessed=2 * query.size * 2, transcendentals=0),
    )(place, parent, live, query, mine, other)


def attend_kernel(first, before, last, arrays, order, starts, query, own, *refs):
    slots = refs[:arrays]
    out, ov, kv, even, odd, zeros, blocks, out_sem = refs[-8:]
    done = refs[arrays] if before else None
    rows, heads, depth = query.shape
    prefix = slots[0].shape[-1]
    width = kv.shape[2]
    base = starts[first]
    end = starts[first + arrays]

    if before:
        from_row, to_row = starts[first - before], base
    else:
        zeros[...] = jnp.zeros_like(zeros)
        from_row, to_row = starts[starts.shape[0] - 1], rows

    @pl.loop(from_row, to_row)
    def _(j):
        pltpu.make_async_copy(done.at[j] if before else zeros, out.at[order[j]], out_sem).start()

    number = jnp.int32(0)
    for s in range(arrays):
        kv[s, :, 0:prefix] = slots[s][...]
        kv[s, :, prefix:width] = own[...]
        lo, hi = starts[first + s], starts[first + s + 1]
        more = (hi - lo + BLOCK - 1) // BLOCK

        def note(b, _):
            blocks[0, number + b] = s
            blocks[1, number + b] = lo + b * BLOCK
            blocks[2, number + b] = jnp.minimum(lo + (b + 1) * BLOCK, hi)
            return 0

        lax.fori_loop(0, more, note, 0)
        number = number + more
    for b in range(2):
        blocks[0, number + b] = 0
        blocks[1, number + b] = rows
        blocks[2, number + b] = rows

    column = lax.broadcasted_iota(jnp.int32, (heads, width - prefix), 1)

    def score(b, to):
        begin = blocks[1, b]
        q = jnp.concatenate([query[order[begin + r]] for r in range(BLOCK)])
        to[...] = jnp.dot(q, kv[blocks[0, b]], preferred_element_type=jnp.float32)

    def finish(b, scores):
        begin = blocks[1, b]
        mine = [
            jnp.where(column == order[begin + r], scores[r * heads:(r + 1) * heads, prefix:width], -jnp.inf)
            for r in range(BLOCK)
        ]
        s = jnp.concatenate([scores[:, 0:prefix], jnp.concatenate(mine)], axis=1)
        top = jnp.max(s, axis=1, keepdims=True)
        expo = jnp.exp2((s - top) * (SCALE * math.log2(math.e)))
        total = jnp.sum(expo, axis=1, keepdims=True)
        weights = (expo * (1.0 / total)).astype(jnp.bfloat16)
        mixed = lax.dot_general(
            weights, kv[blocks[0, b], 0:LAT, :], (((1,), (1,)), ((), ())), preferred_element_type=jnp.float32
        )
        ov[pl.ds(begin, BLOCK)] = mixed.astype(jnp.bfloat16).reshape(BLOCK, heads, LAT)

    def send(b):
        @pl.loop(blocks[1, b], blocks[2, b])
        def _(j):
            pltpu.make_async_copy(ov.at[j], out.at[order[j]], out_sem).start()

    @pl.when(number > 0)
    def _():
        @pl.loop(0, (number + 1) // 2)
        def _(pair):
            b = pair * 2
            score(b, even)
            score(b + 1, odd)
            finish(b, even)
            finish(b + 1, odd)
            if last:
                send(b)
                send(b + 1)

    @pl.loop(from_row, to_row)
    def _(j):
        pltpu.make_async_copy(zeros, out.at[0], out_sem).wait()

    if last:

        @pl.loop(base, end)
        def _(j):
            pltpu.make_async_copy(zeros, out.at[0], out_sem).wait()


def attend(order, starts, first, query, own, slots, before=0, done=None, out=None, last=False):
    rows, heads, depth = query.shape
    count = len(slots)
    prefix = slots[0].shape[-1]
    width = prefix + own.shape[1]
    operands = [order, starts, query, own, *slots] + ([done, out] if before else [])
    work = rows * heads * count // (starts.shape[0] - 1)
    result = jax.ShapeDtypeStruct((rows, heads, LAT), jnp.bfloat16)
    made = pltpu.VMEM((rows + BLOCK, heads, LAT), jnp.bfloat16)
    return pl.pallas_call(
        functools.partial(attend_kernel, first, before, last, count),
        out_shape=result if last else (result, made),
        in_specs=[SMEM, SMEM, VMEM, VMEM] + [VMEM] * count + [VMEM, ANY] * (before > 0),
        out_specs=ANY if last else (ANY, VMEM),
        scratch_shapes=[made] * last + [
            pltpu.VMEM((count, depth, width), jnp.bfloat16),
            pltpu.VMEM((BLOCK * heads, width), jnp.float32),
            pltpu.VMEM((BLOCK * heads, width), jnp.float32),
            pltpu.VMEM((heads, LAT), jnp.bfloat16),
            pltpu.SMEM((3, rows // BLOCK + count + 4), jnp.int32),
            pltpu.SemaphoreType.DMA,
        ],
        input_output_aliases={len(operands) - 1: 0} if before else {},
        compiler_params=pltpu.CompilerParams(vmem_limit_bytes=16 * 1024 * 1024),
        cost_estimate=pl.CostEstimate(
            flops=COST * 2 * work * width * (depth + LAT),
            bytes_accessed=COST * (count * depth * width * 2 + work * LAT * 2),
            transcendentals=COST * work * width,
        ),
    )(*operands)


def ring_of(nodes):
    chips = nodes // 2
    if chips == 8:
        return [0, 2, 4, 6, 7, 5, 3, 1]
    return list(range(chips))


def shards(nodes, child_query, parent_cache, child_latent, parent_place, child_parent, live_rows):
    rows = child_query.shape[0]
    ring = ring_of(nodes)
    chips = len(ring)
    along = [(2 * ring[i], 2 * ring[(i + 1) % chips]) for i in range(chips)]
    along += [(2 * ring[(i + 1) % chips] + 1, 2 * ring[i] + 1) for i in range(chips)]
    across = [(i, i ^ 1) for i in range(nodes)]

    mine = jnp.swapaxes(parent_cache[0], 0, 1)
    other = lax.ppermute(mine, "node", across)
    order, starts, query, kept, other = prepare(
        parent_place, jnp.swapaxes(child_parent, 0, 1), live_rows, child_query, mine, other
    )
    padded = -(-rows // 128) * 128
    pick = jnp.arange(rows)[:, None] == jnp.arange(padded)[None, :]
    own = lax.dot_general(
        child_latent, pick.astype(jnp.bfloat16), (((0,), (0,)), ((), ())), preferred_element_type=jnp.float32
    ).astype(jnp.bfloat16)

    first, result = 0, [None, None]
    phases = [[kept, other]]
    sent = [mine, other]

    def work(phase, last=False):
        nonlocal first, result
        before = 2 if first else 0
        result = attend(order, starts, first, query, own, phases[phase], before, result[1], result[0], last)
        first += 2

    for i in range(1, chips):
        a = forward = lax.ppermute(sent[i - 1], "node", along)
        if i >= 2:
            work(i - 2)
            forward, kept = lax.optimization_barrier((a, result[1]))
            result = result[0], kept
        sent.append(forward)
        phases.append([a, lax.ppermute(a if i + 2 < chips else forward, "node", across)])
    work(chips - 2)
    work(chips - 1, True)
    return result


def solution(mesh):
    return jax.shard_map(
        functools.partial(shards, mesh.shape["node"]),
        mesh=mesh,
        in_specs=(
            P(("groups", "node"), None, None),
            P(("groups", "node"), None, None),
            P(("groups", "node"), None),
            P("groups"),
            P(("groups", "node"), None),
            P(("groups", "node")),
        ),
        out_specs=P(("groups", "node"), None, None),
        check_vma=False,
    )
```

```python
import functools
import math

import jax
import jax.numpy as jnp
from jax import lax
from jax.experimental import pallas as pl
from jax.experimental.pallas import tpu as pltpu
from jax.sharding import PartitionSpec as P

LAT = 512
SCALE = 0.07216878364870322
BLOCK = 6
COST = 4
ANY = pl.BlockSpec(memory_space=pl.ANY)
VMEM = pl.BlockSpec(memory_space=pltpu.VMEM)
SMEM = pl.BlockSpec(memory_space=pltpu.SMEM)


def position_of(chip, chips):
    if chips == 8:
        return jnp.where(chip % 2 == 0, chip // 2, 7 - chip // 2)
    return chip


def slot_of(ahead, same, chips):
    far = jnp.minimum(ahead, chips - ahead)
    slot = 4 * far - 2 + jnp.where(2 * ahead > chips, jnp.where(same, 0, 2), jnp.where(same, 3, 1))
    slot = jnp.where(2 * ahead == chips, 4 * far - 2 + jnp.where(same, 0, 1), slot)
    return jnp.where(ahead == 0, jnp.where(same, 0, 1), slot)


def prepare_kernel(
    place_in, parent_in, live_in, query_in, mine_in, _, plan, query, mine, __, place, parent, live, slots, names, starts, sem
):
    rows = parent.shape[1]
    parents = place.shape[0]
    dead = starts.shape[0] - 1
    chips = parents // 2
    big = [
        pltpu.make_async_copy(query_in, query, sem.at[0]),
        pltpu.make_async_copy(mine_in, mine, sem.at[1]),
    ]
    small = [
        pltpu.make_async_copy(place_in, place, sem.at[2]),
        pltpu.make_async_copy(parent_in, parent, sem.at[3]),
        pltpu.make_async_copy(live_in, live, sem.at[4]),
    ]
    for copy in small + big:
        copy.start()
    for copy in small:
        copy.wait()
    me = lax.axis_index("node")
    core = me % 2
    here = position_of(me // 2, chips)
    alive = live[0]

    def name(p, _):
        at = place[p]
        there = position_of(at // 2, chips)
        ahead = jnp.where(core == 0, there - here, here - there)
        ahead = jnp.where(ahead < 0, ahead + chips, ahead)
        names[p] = slot_of(ahead, at % 2 == core, chips)
        starts[p] = 0
        return 0

    lax.fori_loop(0, parents, name, 0, unroll=4)
    starts[dead] = 0

    def tally(i, _):
        s = jnp.where(i < alive, names[parent[0, i]], dead)
        slots[i] = s
        starts[s] = starts[s] + 1
        return 0

    lax.fori_loop(0, rows, tally, 0, unroll=8)

    def ends(s, total):
        total = total + starts[s]
        starts[s] = total
        return total

    lax.fori_loop(0, dead + 1, ends, jnp.int32(0))

    def put(i, _):
        i = rows - 1 - i
        s = slots[i]
        j = starts[s] - 1
        starts[s] = j
        plan[dead + 1 + j] = i
        return 0

    lax.fori_loop(0, rows, put, 0, unroll=8)
    for i in range(dead + 1 + rows, plan.shape[0]):
        plan[i] = 0

    def tell(s, _):
        plan[s] = starts[s]
        return 0

    lax.fori_loop(0, dead + 1, tell, 0)
    for copy in big:
        copy.wait()


def prepare(place, parent, live, query, mine, other):
    rows, parents = parent.shape[1], place.shape[0]
    return pl.pallas_call(
        prepare_kernel,
        out_shape=(
            jax.ShapeDtypeStruct((parents + 1 + rows + BLOCK,), jnp.int32),
            pltpu.VMEM(query.shape, query.dtype),
            pltpu.VMEM(mine.shape, mine.dtype),
            pltpu.VMEM(other.shape, other.dtype),
        ),
        in_specs=[ANY] * 5 + [VMEM],
        out_specs=(SMEM, VMEM, VMEM, VMEM),
        scratch_shapes=[
            pltpu.SMEM(place.shape, jnp.int32),
            pltpu.SMEM(parent.shape, jnp.int32),
            pltpu.SMEM(live.shape, jnp.int32),
            pltpu.SMEM((rows,), jnp.int32),
            pltpu.SMEM(place.shape, jnp.int32),
            pltpu.SMEM((parents + 1,), jnp.int32),
            pltpu.SemaphoreType.DMA((5,)),
        ],
        input_output_aliases={5: 3},
        compiler_params=pltpu.CompilerParams(vmem_limit_bytes=46 * 1024 * 1024),
        cost_estimate=pl.CostEstimate(flops=0, bytes_accessed=2 * query.size * 2, transcendentals=0),
    )(place, parent, live, query, mine, other)


def attend_kernel(first, before, last, arrays, plan, query, own, *refs):
    slots = refs[:arrays]
    out, ov, kv, even, odd, zeros, blocks, out_sem = refs[-8:]
    done = refs[arrays] if before else None
    rows, heads, depth = query.shape
    prefix = slots[0].shape[-1]
    width = kv.shape[2]
    dead = plan.shape[0] - BLOCK - rows - 1
    order = plan.at[pl.ds(dead + 1, rows + BLOCK)]
    starts = plan.at[pl.ds(0, dead + 1)]
    base = starts[first]
    end = starts[first + arrays]

    if before:
        from_row, to_row = starts[first - before], base
    else:
        zeros[...] = jnp.zeros_like(zeros)
        from_row, to_row = starts[dead], rows

    @pl.loop(from_row, to_row)
    def _(j):
        pltpu.make_async_copy(done.at[j] if before else zeros, out.at[order[j]], out_sem).start()

    number = jnp.int32(0)
    for s in range(arrays):
        kv[s, :, 0:prefix] = slots[s][...]
        kv[s, :, prefix:width] = own[...]
        lo, hi = starts[first + s], starts[first + s + 1]
        more = (hi - lo + BLOCK - 1) // BLOCK

        def note(b, _):
            blocks[0, number + b] = s
            blocks[1, number + b] = lo + b * BLOCK
            blocks[2, number + b] = jnp.minimum(lo + (b + 1) * BLOCK, hi)
            return 0

        lax.fori_loop(0, more, note, 0)
        number = number + more
    column = lax.broadcasted_iota(jnp.int32, (heads, width - prefix), 1)

    def score(b, to):
        begin = blocks[1, b]
        q = jnp.concatenate([query[order[begin + r]] for r in range(BLOCK)])
        to[...] = jnp.dot(q, kv[blocks[0, b]], preferred_element_type=jnp.float32)

    def finish(b, scores):
        begin = blocks[1, b]
        mine = [
            jnp.where(column == order[begin + r], scores[r * heads:(r + 1) * heads, prefix:width], -jnp.inf)
            for r in range(BLOCK)
        ]
        s = jnp.concatenate([scores[:, 0:prefix], jnp.concatenate(mine)], axis=1)
        top = jnp.max(s, axis=1, keepdims=True)
        expo = jnp.exp2((s - top) * (SCALE * math.log2(math.e)))
        total = jnp.sum(expo, axis=1, keepdims=True)
        weights = (expo * (1.0 / total)).astype(jnp.bfloat16)
        mixed = lax.dot_general(
            weights, kv[blocks[0, b], 0:LAT, :], (((1,), (1,)), ((), ())), preferred_element_type=jnp.float32
        )
        ov[pl.ds(begin, BLOCK)] = mixed.astype(jnp.bfloat16).reshape(BLOCK, heads, LAT)

    def send(b):
        @pl.loop(blocks[1, b], blocks[2, b])
        def _(j):
            pltpu.make_async_copy(ov.at[j], out.at[order[j]], out_sem).start()

    @pl.loop(0, number // 2)
    def _(pair):
        b = pair * 2
        score(b, even)
        score(b + 1, odd)
        finish(b, even)
        finish(b + 1, odd)
        if last:
            send(b)
            send(b + 1)

    @pl.when(number % 2 == 1)
    def _():
        score(number - 1, even)
        finish(number - 1, even)
        if last:
            send(number - 1)

    @pl.loop(from_row, to_row)
    def _(j):
        pltpu.make_async_copy(zeros, out.at[0], out_sem).wait()

    if last:

        @pl.loop(base, end)
        def _(j):
            pltpu.make_async_copy(zeros, out.at[0], out_sem).wait()


def attend(plan, first, query, own, slots, before=0, done=None, out=None, last=False):
    rows, heads, depth = query.shape
    count = len(slots)
    prefix = slots[0].shape[-1]
    width = prefix + own.shape[1]
    operands = [plan, query, own, *slots] + ([done, out] if before else [])
    work = rows * heads * count // (plan.shape[0] - BLOCK - rows - 1)
    result = jax.ShapeDtypeStruct((rows, heads, LAT), jnp.bfloat16)
    made = pltpu.VMEM((rows + BLOCK, heads, LAT), jnp.bfloat16)
    return pl.pallas_call(
        functools.partial(attend_kernel, first, before, last, count),
        out_shape=result if last else (result, made),
        in_specs=[SMEM, VMEM, VMEM] + [VMEM] * count + [VMEM, ANY] * (before > 0),
        out_specs=ANY if last else (ANY, VMEM),
        scratch_shapes=[made] * last + [
            pltpu.VMEM((count, depth, width), jnp.bfloat16),
            pltpu.VMEM((BLOCK * heads, width), jnp.float32),
            pltpu.VMEM((BLOCK * heads, width), jnp.float32),
            pltpu.VMEM((heads, LAT), jnp.bfloat16),
            pltpu.SMEM((3, rows // BLOCK + count + 4), jnp.int32),
            pltpu.SemaphoreType.DMA,
        ],
        input_output_aliases={len(operands) - 1: 0} if before else {},
        compiler_params=pltpu.CompilerParams(vmem_limit_bytes=16 * 1024 * 1024),
        cost_estimate=pl.CostEstimate(
            flops=COST * 2 * work * width * (depth + LAT),
            bytes_accessed=COST * (count * depth * width * 2 + work * LAT * 2),
            transcendentals=COST * work * width,
        ),
    )(*operands)


def ring_of(nodes):
    chips = nodes // 2
    if chips == 8:
        return [0, 2, 4, 6, 7, 5, 3, 1]
    return list(range(chips))


def shards(nodes, child_query, parent_cache, child_latent, parent_place, child_parent, live_rows):
    rows = child_query.shape[0]
    ring = ring_of(nodes)
    chips = len(ring)
    along = [(2 * ring[i], 2 * ring[(i + 1) % chips]) for i in range(chips)]
    along += [(2 * ring[(i + 1) % chips] + 1, 2 * ring[i] + 1) for i in range(chips)]
    across = [(i, i ^ 1) for i in range(nodes)]

    mine = jnp.swapaxes(parent_cache[0], 0, 1)
    other = lax.ppermute(mine, "node", across)
    plan, query, kept, other = prepare(
        parent_place, jnp.swapaxes(child_parent, 0, 1), live_rows, child_query, mine, other
    )
    padded = -(-rows // 128) * 128
    pick = jnp.arange(rows)[:, None] == jnp.arange(padded)[None, :]
    own = lax.dot_general(
        child_latent, pick.astype(jnp.bfloat16), (((0,), (0,)), ((), ())), preferred_element_type=jnp.float32
    ).astype(jnp.bfloat16)

    first, result = 0, (None, None)
    phases = [[kept, other]]
    sent = [mine, other]

    def work(phase, last=False):
        nonlocal first, result
        before = 2 if first else 0
        result = attend(plan, first, query, own, phases[phase], before, result[1], result[0], last)
        first += 2

    for i in range(1, chips):
        a = forward = lax.ppermute(sent[i - 1], "node", along)
        if i >= 2:
            work(i - 2)
            forward, done = lax.optimization_barrier((a, result[1]))
            result = result[0], done
        sent.append(forward)
        phases.append([a, lax.ppermute(forward, "node", across)])
    work(chips - 2)
    work(chips - 1, True)
    return result


def solution(mesh):
    return jax.shard_map(
        functools.partial(shards, mesh.shape["node"]),
        mesh=mesh,
        in_specs=(
            P(("groups", "node"), None, None),
            P(("groups", "node"), None, None),
            P(("groups", "node"), None),
            P("groups"),
            P(("groups", "node"), None),
            P(("groups", "node")),
        ),
        out_specs=P(("groups", "node"), None, None),
        check_vma=False,
    )
```

```python
import functools
import math

import jax
import jax.numpy as jnp
from jax import lax
from jax.experimental import pallas as pl
from jax.experimental.pallas import tpu as pltpu
from jax.sharding import PartitionSpec as P

LAT = 512
SCALE = 0.07216878364870322
BLOCK = 6
COST = 4
FIRST = 1
ANY = pl.BlockSpec(memory_space=pl.ANY)
VMEM = pl.BlockSpec(memory_space=pltpu.VMEM)
SMEM = pl.BlockSpec(memory_space=pltpu.SMEM)


def position_of(chip, chips):
    if chips == 8:
        return jnp.where(chip % 2 == 0, chip // 2, 7 - chip // 2)
    return chip


def slot_of(ahead, same, chips):
    far = jnp.minimum(ahead, chips - ahead)
    slot = 4 * far - 2 + jnp.where(2 * ahead > chips, jnp.where(same, 0, 2), jnp.where(same, 3, 1))
    slot = jnp.where(2 * ahead == chips, 4 * far - 2 + jnp.where(same, 0, 1), slot)
    return jnp.where(ahead == 0, jnp.where(same, 0, 1), slot)


def prepare_kernel(
    place_in, parent_in, live_in, query_in, mine_in, plan, query, mine, place, parent, live, slots, names, starts, sem
):
    rows = parent.shape[1]
    parents = place.shape[0]
    dead = starts.shape[0] - 1
    chips = parents // 2
    big = [
        pltpu.make_async_copy(query_in, query, sem.at[0]),
        pltpu.make_async_copy(mine_in, mine, sem.at[1]),
    ]
    small = [
        pltpu.make_async_copy(place_in, place, sem.at[2]),
        pltpu.make_async_copy(parent_in, parent, sem.at[3]),
        pltpu.make_async_copy(live_in, live, sem.at[4]),
    ]
    for copy in small + big:
        copy.start()
    for copy in small:
        copy.wait()
    me = lax.axis_index("node")
    core = me % 2
    here = position_of(me // 2, chips)
    alive = live[0]

    def name(p, _):
        at = place[p]
        there = position_of(at // 2, chips)
        ahead = jnp.where(core == 0, there - here, here - there)
        ahead = jnp.where(ahead < 0, ahead + chips, ahead)
        names[p] = slot_of(ahead, at % 2 == core, chips)
        starts[p] = 0
        return 0

    lax.fori_loop(0, parents, name, 0, unroll=4)
    starts[dead] = 0

    def tally(i, _):
        s = jnp.where(i < alive, names[parent[0, i]], dead)
        slots[i] = s
        starts[s] = starts[s] + 1
        return 0

    lax.fori_loop(0, rows, tally, 0, unroll=8)

    def ends(s, total):
        total = total + starts[s]
        starts[s] = total
        return total

    lax.fori_loop(0, dead + 1, ends, jnp.int32(0))

    def put(i, _):
        i = rows - 1 - i
        s = slots[i]
        j = starts[s] - 1
        starts[s] = j
        plan[dead + 1 + j] = i
        return 0

    lax.fori_loop(0, rows, put, 0, unroll=8)
    for i in range(dead + 1 + rows, plan.shape[0]):
        plan[i] = 0

    def tell(s, _):
        plan[s] = starts[s]
        return 0

    lax.fori_loop(0, dead + 1, tell, 0)
    for copy in big:
        copy.wait()


def prepare(place, parent, live, query, mine):
    rows, parents = parent.shape[1], place.shape[0]
    return pl.pallas_call(
        prepare_kernel,
        out_shape=(
            jax.ShapeDtypeStruct((parents + 1 + rows + BLOCK,), jnp.int32),
            pltpu.VMEM(query.shape, query.dtype),
            pltpu.VMEM(mine.shape, mine.dtype),
        ),
        in_specs=[ANY] * 5,
        out_specs=(SMEM, VMEM, VMEM),
        scratch_shapes=[
            pltpu.SMEM(place.shape, jnp.int32),
            pltpu.SMEM(parent.shape, jnp.int32),
            pltpu.SMEM(live.shape, jnp.int32),
            pltpu.SMEM((rows,), jnp.int32),
            pltpu.SMEM(place.shape, jnp.int32),
            pltpu.SMEM((parents + 1,), jnp.int32),
            pltpu.SemaphoreType.DMA((5,)),
        ],
        compiler_params=pltpu.CompilerParams(vmem_limit_bytes=48 * 1024 * 1024),
        cost_estimate=pl.CostEstimate(flops=0, bytes_accessed=2 * query.size * 2, transcendentals=0),
    )(place, parent, live, query, mine)


def attend_kernel(first, before, last, arrays, plan, query, own, *refs):
    slots = refs[:arrays]
    out, ov, kv, even, odd, zeros, blocks, out_sem = refs[-8:]
    done = refs[arrays] if before else None
    rows, heads, depth = query.shape
    prefix = slots[0].shape[-1]
    width = kv.shape[2]
    dead = plan.shape[0] - BLOCK - rows - 1
    order = plan.at[pl.ds(dead + 1, rows + BLOCK)]
    starts = plan.at[pl.ds(0, dead + 1)]
    base = starts[first]
    end = starts[first + arrays]

    if before:
        from_row, to_row = starts[first - before], base
    else:
        zeros[...] = jnp.zeros_like(zeros)
        from_row, to_row = starts[dead], rows

    @pl.loop(from_row, to_row)
    def _(j):
        pltpu.make_async_copy(done.at[j] if before else zeros, out.at[order[j]], out_sem).start()

    number = jnp.int32(0)
    for s in range(arrays):
        kv[s, :, 0:prefix] = slots[s][...]
        kv[s, :, prefix:width] = own[...]
        lo, hi = starts[first + s], starts[first + s + 1]
        more = (hi - lo + BLOCK - 1) // BLOCK

        def note(b, _):
            blocks[0, number + b] = s
            blocks[1, number + b] = lo + b * BLOCK
            blocks[2, number + b] = jnp.minimum(lo + (b + 1) * BLOCK, hi)
            return 0

        lax.fori_loop(0, more, note, 0)
        number = number + more
    column = lax.broadcasted_iota(jnp.int32, (heads, width - prefix), 1)

    def score(b, to):
        begin = blocks[1, b]
        q = jnp.concatenate([query[order[begin + r]] for r in range(BLOCK)])
        to[...] = jnp.dot(q, kv[blocks[0, b]], preferred_element_type=jnp.float32)

    def finish(b, scores):
        begin = blocks[1, b]
        mine = [
            jnp.where(column == order[begin + r], scores[r * heads:(r + 1) * heads, prefix:width], -jnp.inf)
            for r in range(BLOCK)
        ]
        s = jnp.concatenate([scores[:, 0:prefix], jnp.concatenate(mine)], axis=1)
        top = jnp.max(s, axis=1, keepdims=True)
        expo = jnp.exp2((s - top) * (SCALE * math.log2(math.e)))
        total = jnp.sum(expo, axis=1, keepdims=True)
        weights = (expo * (1.0 / total)).astype(jnp.bfloat16)
        mixed = lax.dot_general(
            weights, kv[blocks[0, b], 0:LAT, :], (((1,), (1,)), ((), ())), preferred_element_type=jnp.float32
        )
        ov[pl.ds(begin, BLOCK)] = mixed.astype(jnp.bfloat16).reshape(BLOCK, heads, LAT)

    def send(b):
        @pl.loop(blocks[1, b], blocks[2, b])
        def _(j):
            pltpu.make_async_copy(ov.at[j], out.at[order[j]], out_sem).start()

    @pl.loop(0, number // 2)
    def _(pair):
        b = pair * 2
        score(b, even)
        score(b + 1, odd)
        finish(b, even)
        finish(b + 1, odd)
        if last:
            send(b)
            send(b + 1)

    @pl.when(number % 2 == 1)
    def _():
        score(number - 1, even)
        finish(number - 1, even)
        if last:
            send(number - 1)

    @pl.loop(from_row, to_row)
    def _(j):
        pltpu.make_async_copy(zeros, out.at[0], out_sem).wait()

    if last:

        @pl.loop(base, end)
        def _(j):
            pltpu.make_async_copy(zeros, out.at[0], out_sem).wait()


def attend(plan, first, query, own, slots, before=0, done=None, out=None, last=False, cost=COST):
    rows, heads, depth = query.shape
    count = len(slots)
    prefix = slots[0].shape[-1]
    width = prefix + own.shape[1]
    operands = [plan, query, own, *slots] + ([done, out] if before else [])
    work = rows * heads * count // (plan.shape[0] - BLOCK - rows - 1)
    result = jax.ShapeDtypeStruct((rows, heads, LAT), jnp.bfloat16)
    made = pltpu.VMEM((rows + BLOCK, heads, LAT), jnp.bfloat16)
    return pl.pallas_call(
        functools.partial(attend_kernel, first, before, last, count),
        out_shape=result if last else (result, made),
        in_specs=[SMEM, VMEM, VMEM] + [VMEM] * count + [VMEM, ANY] * (before > 0),
        out_specs=ANY if last else (ANY, VMEM),
        scratch_shapes=[made] * last + [
            pltpu.VMEM((count, depth, width), jnp.bfloat16),
            pltpu.VMEM((BLOCK * heads, width), jnp.float32),
            pltpu.VMEM((BLOCK * heads, width), jnp.float32),
            pltpu.VMEM((heads, LAT), jnp.bfloat16),
            pltpu.SMEM((3, rows // BLOCK + count + 4), jnp.int32),
            pltpu.SemaphoreType.DMA,
        ],
        input_output_aliases={len(operands) - 1: 0} if before else {},
        compiler_params=pltpu.CompilerParams(vmem_limit_bytes=16 * 1024 * 1024),
        cost_estimate=pl.CostEstimate(
            flops=cost * 2 * work * width * (depth + LAT),
            bytes_accessed=cost * (count * depth * width * 2 + work * LAT * 2),
            transcendentals=cost * work * width,
        ),
    )(*operands)


def ring_of(nodes):
    chips = nodes // 2
    if chips == 8:
        return [0, 2, 4, 6, 7, 5, 3, 1]
    return list(range(chips))


def shards(nodes, child_query, parent_cache, child_latent, parent_place, child_parent, live_rows):
    rows = child_query.shape[0]
    ring = ring_of(nodes)
    chips = len(ring)
    along = [(2 * ring[i], 2 * ring[(i + 1) % chips]) for i in range(chips)]
    along += [(2 * ring[(i + 1) % chips] + 1, 2 * ring[i] + 1) for i in range(chips)]
    across = [(i, i ^ 1) for i in range(nodes)]

    mine = jnp.swapaxes(parent_cache[0], 0, 1)
    other = lax.ppermute(mine, "node", across)
    other, place = lax.optimization_barrier((other, parent_place))
    plan, query, kept = prepare(place, jnp.swapaxes(child_parent, 0, 1), live_rows, child_query, mine)
    padded = -(-rows // 128) * 128
    pick = jnp.arange(rows)[:, None] == jnp.arange(padded)[None, :]
    own = lax.dot_general(
        child_latent, pick.astype(jnp.bfloat16), (((0,), (0,)), ((), ())), preferred_element_type=jnp.float32
    ).astype(jnp.bfloat16)

    first, result = 0, (None, None)
    phases = [[kept, other]]
    sent = [mine, other]

    def work(phase, last=False):
        nonlocal first, result
        before = 2 if first else 0
        result = attend(plan, first, query, own, phases[phase], before, result[1], result[0], last, COST if first else FIRST)
        first += 2

    for i in range(1, chips):
        a = forward = lax.ppermute(sent[i - 1], "node", along)
        if i == 1:
            forward, plan = lax.optimization_barrier((a, plan))
        if i >= 2:
            work(i - 2)
            forward, done = lax.optimization_barrier((a, result[1]))
            result = result[0], done
        sent.append(forward)
        phases.append([a, lax.ppermute(forward, "node", across)])
    work(chips - 2)
    work(chips - 1, True)
    return result


def solution(mesh):
    return jax.shard_map(
        functools.partial(shards, mesh.shape["node"]),
        mesh=mesh,
        in_specs=(
            P(("groups", "node"), None, None),
            P(("groups", "node"), None, None),
            P(("groups", "node"), None),
            P("groups"),
            P(("groups", "node"), None),
            P(("groups", "node")),
        ),
        out_specs=P(("groups", "node"), None, None),
        check_vma=False,
    )
```

```python
import functools
import math

import jax
import jax.numpy as jnp
from jax import lax
from jax.experimental import pallas as pl
from jax.experimental.pallas import tpu as pltpu
from jax.sharding import PartitionSpec as P

LAT = 512
SCALE = 0.07216878364870322
BLOCK = 6
COST = 4
FIRST = 1
ANY = pl.BlockSpec(memory_space=pl.ANY)
VMEM = pl.BlockSpec(memory_space=pltpu.VMEM)
SMEM = pl.BlockSpec(memory_space=pltpu.SMEM)


def position_of(chip, chips):
    if chips == 8:
        return jnp.where(chip % 2 == 0, chip // 2, 7 - chip // 2)
    return chip


def slot_of(ahead, same, chips):
    far = jnp.minimum(ahead, chips - ahead)
    slot = 4 * far - 2 + jnp.where(2 * ahead > chips, jnp.where(same, 0, 2), jnp.where(same, 3, 1))
    slot = jnp.where(2 * ahead == chips, 4 * far - 2 + jnp.where(same, 0, 1), slot)
    return jnp.where(ahead == 0, jnp.where(same, 0, 1), slot)


def prepare_kernel(
    place_in, parent_in, live_in, query_in, mine_in, plan, query, mine, place, parent, live, slots, names, starts, sem
):
    rows = parent.shape[1]
    parents = place.shape[0]
    dead = starts.shape[0] - 1
    chips = parents // 2
    big = [
        pltpu.make_async_copy(query_in, query, sem.at[0]),
        pltpu.make_async_copy(mine_in, mine, sem.at[1]),
    ]
    small = [
        pltpu.make_async_copy(place_in, place, sem.at[2]),
        pltpu.make_async_copy(parent_in, parent, sem.at[3]),
        pltpu.make_async_copy(live_in, live, sem.at[4]),
    ]
    for copy in small + big:
        copy.start()
    for copy in small:
        copy.wait()
    me = lax.axis_index("node")
    core = me % 2
    here = position_of(me // 2, chips)
    alive = live[0]

    def name(p, _):
        at = place[p]
        there = position_of(at // 2, chips)
        ahead = jnp.where(core == 0, there - here, here - there)
        ahead = jnp.where(ahead < 0, ahead + chips, ahead)
        names[p] = slot_of(ahead, at % 2 == core, chips)
        starts[p] = 0
        return 0

    lax.fori_loop(0, parents, name, 0, unroll=4)
    starts[dead] = 0

    def tally(i, _):
        s = jnp.where(i < alive, names[parent[0, i]], dead)
        slots[i] = s
        starts[s] = starts[s] + 1
        return 0

    lax.fori_loop(0, rows, tally, 0, unroll=8)

    def ends(s, total):
        total = total + starts[s]
        starts[s] = total
        return total

    lax.fori_loop(0, dead + 1, ends, jnp.int32(0))

    def put(i, _):
        i = rows - 1 - i
        s = slots[i]
        j = starts[s] - 1
        starts[s] = j
        plan[dead + 1 + j] = i
        return 0

    lax.fori_loop(0, rows, put, 0, unroll=8)
    for i in range(dead + 1 + rows, plan.shape[0]):
        plan[i] = 0

    def tell(s, _):
        plan[s] = starts[s]
        return 0

    lax.fori_loop(0, dead + 1, tell, 0)
    for copy in big:
        copy.wait()


def prepare(place, parent, live, query, mine):
    rows, parents = parent.shape[1], place.shape[0]
    return pl.pallas_call(
        prepare_kernel,
        out_shape=(
            jax.ShapeDtypeStruct((parents + 1 + rows + BLOCK,), jnp.int32),
            pltpu.VMEM(query.shape, query.dtype),
            pltpu.VMEM(mine.shape, mine.dtype),
        ),
        in_specs=[ANY] * 5,
        out_specs=(SMEM, VMEM, VMEM),
        scratch_shapes=[
            pltpu.SMEM(place.shape, jnp.int32),
            pltpu.SMEM(parent.shape, jnp.int32),
            pltpu.SMEM(live.shape, jnp.int32),
            pltpu.SMEM((rows,), jnp.int32),
            pltpu.SMEM(place.shape, jnp.int32),
            pltpu.SMEM((parents + 1,), jnp.int32),
            pltpu.SemaphoreType.DMA((5,)),
        ],
        compiler_params=pltpu.CompilerParams(vmem_limit_bytes=48 * 1024 * 1024),
        cost_estimate=pl.CostEstimate(flops=0, bytes_accessed=2 * query.size * 2, transcendentals=0),
    )(place, parent, live, query, mine)


def attend_kernel(first, before, last, arrays, plan, query, own, *refs):
    slots = refs[:arrays]
    out, ov, kv, even, odd, zeros, blocks, out_sem = refs[-8:]
    done = refs[arrays] if before else None
    rows, heads, depth = query.shape
    prefix = slots[0].shape[-1]
    width = kv.shape[2]
    dead = plan.shape[0] - BLOCK - rows - 1
    order = plan.at[pl.ds(dead + 1, rows + BLOCK)]
    starts = plan.at[pl.ds(0, dead + 1)]
    base = starts[first]
    end = starts[first + arrays]

    if before:
        from_row, to_row = starts[first - before], base
    else:
        zeros[...] = jnp.zeros_like(zeros)
        from_row, to_row = starts[dead], rows

    @pl.loop(from_row, to_row)
    def _(j):
        pltpu.make_async_copy(done.at[j] if before else zeros, out.at[order[j]], out_sem).start()

    number = jnp.int32(0)
    for s in range(arrays):
        kv[s, :, 0:prefix] = slots[s][...]
        kv[s, :, prefix:width] = own[...]
        lo, hi = starts[first + s], starts[first + s + 1]
        more = (hi - lo + BLOCK - 1) // BLOCK

        def note(b, _):
            blocks[0, number + b] = s
            blocks[1, number + b] = lo + b * BLOCK
            blocks[2, number + b] = jnp.minimum(lo + (b + 1) * BLOCK, hi)
            return 0

        lax.fori_loop(0, more, note, 0)
        number = number + more
    column = lax.broadcasted_iota(jnp.int32, (heads, width - prefix), 1)

    def score(b, to):
        begin = blocks[1, b]
        q = jnp.concatenate([query[order[begin + r]] for r in range(BLOCK)])
        to[...] = jnp.dot(q, kv[blocks[0, b]], preferred_element_type=jnp.float32)

    def finish(b, scores):
        begin = blocks[1, b]
        mine = [
            jnp.where(column == order[begin + r], scores[r * heads:(r + 1) * heads, prefix:width], -jnp.inf)
            for r in range(BLOCK)
        ]
        s = jnp.concatenate([scores[:, 0:prefix], jnp.concatenate(mine)], axis=1)
        top = jnp.max(s, axis=1, keepdims=True)
        expo = jnp.exp2((s - top) * (SCALE * math.log2(math.e)))
        total = jnp.sum(expo, axis=1, keepdims=True)
        weights = (expo * (1.0 / total)).astype(jnp.bfloat16)
        mixed = lax.dot_general(
            weights, kv[blocks[0, b], 0:LAT, :], (((1,), (1,)), ((), ())), preferred_element_type=jnp.float32
        )
        ov[pl.ds(begin, BLOCK)] = mixed.astype(jnp.bfloat16).reshape(BLOCK, heads, LAT)

    def send(b):
        @pl.loop(blocks[1, b], blocks[2, b])
        def _(j):
            pltpu.make_async_copy(ov.at[j], out.at[order[j]], out_sem).start()

    @pl.loop(0, number // 2)
    def _(pair):
        b = pair * 2
        score(b, even)
        score(b + 1, odd)
        finish(b, even)
        finish(b + 1, odd)
        if last:
            send(b)
            send(b + 1)

    @pl.when(number % 2 == 1)
    def _():
        score(number - 1, even)
        finish(number - 1, even)
        if last:
            send(number - 1)

    @pl.loop(from_row, to_row)
    def _(j):
        pltpu.make_async_copy(zeros, out.at[0], out_sem).wait()

    if last:

        @pl.loop(base, end)
        def _(j):
            pltpu.make_async_copy(zeros, out.at[0], out_sem).wait()


def attend(plan, first, query, own, slots, before=0, done=None, out=None, last=False, cost=COST):
    rows, heads, depth = query.shape
    count = len(slots)
    prefix = slots[0].shape[-1]
    width = prefix + own.shape[1]
    operands = [plan, query, own, *slots] + ([done, out] if before else [])
    work = rows * heads * count // (plan.shape[0] - BLOCK - rows - 1)
    result = jax.ShapeDtypeStruct((rows, heads, LAT), jnp.bfloat16)
    made = pltpu.VMEM((rows + BLOCK, heads, LAT), jnp.bfloat16)
    return pl.pallas_call(
        functools.partial(attend_kernel, first, before, last, count),
        out_shape=result if last else (result, made),
        in_specs=[SMEM, VMEM, VMEM] + [VMEM] * count + [VMEM, ANY] * (before > 0),
        out_specs=ANY if last else (ANY, VMEM),
        scratch_shapes=[made] * last + [
            pltpu.VMEM((count, depth, width), jnp.bfloat16),
            pltpu.VMEM((BLOCK * heads, width), jnp.float32),
            pltpu.VMEM((BLOCK * heads, width), jnp.float32),
            pltpu.VMEM((heads, LAT), jnp.bfloat16),
            pltpu.SMEM((3, rows // BLOCK + count + 4), jnp.int32),
            pltpu.SemaphoreType.DMA,
        ],
        input_output_aliases={len(operands) - 1: 0} if before else {},
        compiler_params=pltpu.CompilerParams(vmem_limit_bytes=16 * 1024 * 1024),
        cost_estimate=pl.CostEstimate(
            flops=cost * 2 * work * width * (depth + LAT),
            bytes_accessed=cost * (count * depth * width * 2 + work * LAT * 2),
            transcendentals=cost * work * width,
        ),
    )(*operands)


def ring_of(nodes):
    chips = nodes // 2
    if chips == 8:
        return [0, 2, 4, 6, 7, 5, 3, 1]
    return list(range(chips))


def shards(nodes, child_query, parent_cache, child_latent, parent_place, child_parent, live_rows):
    rows = child_query.shape[0]
    ring = ring_of(nodes)
    chips = len(ring)
    along = [(2 * ring[i], 2 * ring[(i + 1) % chips]) for i in range(chips)]
    along += [(2 * ring[(i + 1) % chips] + 1, 2 * ring[i] + 1) for i in range(chips)]
    across = [(i, i ^ 1) for i in range(nodes)]

    mine = jnp.swapaxes(parent_cache[0], 0, 1)
    other = lax.ppermute(mine, "node", across)
    other, place = lax.optimization_barrier((other, parent_place))
    plan, query, kept = prepare(place, jnp.swapaxes(child_parent, 0, 1), live_rows, child_query, mine)
    padded = -(-rows // 128) * 128
    pick = jnp.arange(rows)[:, None] == jnp.arange(padded)[None, :]
    own = lax.dot_general(
        child_latent, pick.astype(jnp.bfloat16), (((0,), (0,)), ((), ())), preferred_element_type=jnp.float32
    ).astype(jnp.bfloat16)

    first, result = 0, (None, None)
    phases = [[kept, other]]
    sent = [mine, other]

    def work(phase, last=False):
        nonlocal first, result
        before = len(phases[phase - 1]) if first else 0
        result = attend(plan, first, query, own, phases[phase], before, result[1], result[0], last, COST if first else FIRST)
        first += len(phases[phase])

    for i in range(1, chips):
        a = forward = lax.ppermute(sent[i - 1], "node", along)
        if i == 1:
            forward, plan = lax.optimization_barrier((a, plan))
        if i >= 2:
            if i == chips - 1:
                phases[i - 2].append(phases[i - 1].pop(0))
            work(i - 2)
            forward, done = lax.optimization_barrier((a, result[1]))
            result = result[0], done
        sent.append(forward)
        phases.append([a, lax.ppermute(forward, "node", across)])
    phases[-2].append(phases[-1].pop(0))
    work(chips - 2)
    work(chips - 1, True)
    return result


def solution(mesh):
    return jax.shard_map(
        functools.partial(shards, mesh.shape["node"]),
        mesh=mesh,
        in_specs=(
            P(("groups", "node"), None, None),
            P(("groups", "node"), None, None),
            P(("groups", "node"), None),
            P("groups"),
            P(("groups", "node"), None),
            P(("groups", "node")),
        ),
        out_specs=P(("groups", "node"), None, None),
        check_vma=False,
    )
```

```python
import functools
import math

import jax
import jax.numpy as jnp
from jax import lax
from jax.experimental import pallas as pl
from jax.experimental.pallas import tpu as pltpu
from jax.sharding import PartitionSpec as P

LAT = 512
SCALE = 0.07216878364870322
BLOCK = 5
COST = 4
FIRST = 1
ANY = pl.BlockSpec(memory_space=pl.ANY)
VMEM = pl.BlockSpec(memory_space=pltpu.VMEM)
SMEM = pl.BlockSpec(memory_space=pltpu.SMEM)


def position_of(chip, chips):
    if chips == 8:
        return jnp.where(chip % 2 == 0, chip // 2, 7 - chip // 2)
    return chip


def slot_of(ahead, same, chips):
    far = jnp.minimum(ahead, chips - ahead)
    slot = 4 * far - 2 + jnp.where(2 * ahead > chips, jnp.where(same, 0, 2), jnp.where(same, 3, 1))
    slot = jnp.where(2 * ahead == chips, 4 * far - 2 + jnp.where(same, 0, 1), slot)
    return jnp.where(ahead == 0, jnp.where(same, 0, 1), slot)


def prepare_kernel(
    place_in, parent_in, live_in, query_in, mine_in, plan, query, mine, place, parent, live, slots, names, starts, sem
):
    rows = parent.shape[1]
    parents = place.shape[0]
    dead = starts.shape[0] - 1
    chips = parents // 2
    big = [
        pltpu.make_async_copy(query_in, query, sem.at[0]),
        pltpu.make_async_copy(mine_in, mine, sem.at[1]),
    ]
    small = [
        pltpu.make_async_copy(place_in, place, sem.at[2]),
        pltpu.make_async_copy(parent_in, parent, sem.at[3]),
        pltpu.make_async_copy(live_in, live, sem.at[4]),
    ]
    for copy in small + big:
        copy.start()
    for copy in small:
        copy.wait()
    me = lax.axis_index("node")
    core = me % 2
    here = position_of(me // 2, chips)
    alive = live[0]

    def name(p, _):
        at = place[p]
        there = position_of(at // 2, chips)
        ahead = jnp.where(core == 0, there - here, here - there)
        ahead = jnp.where(ahead < 0, ahead + chips, ahead)
        names[p] = slot_of(ahead, at % 2 == core, chips)
        starts[p] = 0
        return 0

    lax.fori_loop(0, parents, name, 0, unroll=4)
    starts[dead] = 0

    def tally(i, _):
        s = jnp.where(i < alive, names[parent[0, i]], dead)
        slots[i] = s
        starts[s] = starts[s] + 1
        return 0

    lax.fori_loop(0, rows, tally, 0, unroll=8)

    def ends(s, total):
        total = total + starts[s]
        starts[s] = total
        return total

    lax.fori_loop(0, dead + 1, ends, jnp.int32(0))

    def put(i, _):
        i = rows - 1 - i
        s = slots[i]
        j = starts[s] - 1
        starts[s] = j
        plan[dead + 1 + j] = i
        return 0

    lax.fori_loop(0, rows, put, 0, unroll=8)
    for i in range(dead + 1 + rows, plan.shape[0]):
        plan[i] = 0

    def tell(s, _):
        plan[s] = starts[s]
        return 0

    lax.fori_loop(0, dead + 1, tell, 0)
    for copy in big:
        copy.wait()


def prepare(place, parent, live, query, mine):
    rows, parents = parent.shape[1], place.shape[0]
    return pl.pallas_call(
        prepare_kernel,
        out_shape=(
            jax.ShapeDtypeStruct((parents + 1 + rows + BLOCK,), jnp.int32),
            pltpu.VMEM(query.shape, query.dtype),
            pltpu.VMEM(mine.shape, mine.dtype),
        ),
        in_specs=[ANY] * 5,
        out_specs=(SMEM, VMEM, VMEM),
        scratch_shapes=[
            pltpu.SMEM(place.shape, jnp.int32),
            pltpu.SMEM(parent.shape, jnp.int32),
            pltpu.SMEM(live.shape, jnp.int32),
            pltpu.SMEM((rows,), jnp.int32),
            pltpu.SMEM(place.shape, jnp.int32),
            pltpu.SMEM((parents + 1,), jnp.int32),
            pltpu.SemaphoreType.DMA((5,)),
        ],
        compiler_params=pltpu.CompilerParams(vmem_limit_bytes=48 * 1024 * 1024),
        cost_estimate=pl.CostEstimate(flops=0, bytes_accessed=2 * query.size * 2, transcendentals=0),
    )(place, parent, live, query, mine)


def attend_kernel(first, before, last, arrays, plan, query, own, *refs):
    slots = refs[:arrays]
    out, ov, kv, even, odd, zeros, blocks, out_sem = refs[-8:]
    done = refs[arrays] if before else None
    rows, heads, depth = query.shape
    prefix = slots[0].shape[-1]
    width = kv.shape[2]
    dead = plan.shape[0] - BLOCK - rows - 1
    order = plan.at[pl.ds(dead + 1, rows + BLOCK)]
    starts = plan.at[pl.ds(0, dead + 1)]
    base = starts[first]
    end = starts[first + arrays]

    if before:
        from_row, to_row = starts[first - before], base
    else:
        zeros[...] = jnp.zeros_like(zeros)
        from_row, to_row = starts[dead], rows

    @pl.loop(from_row, to_row)
    def _(j):
        pltpu.make_async_copy(done.at[j] if before else zeros, out.at[order[j]], out_sem).start()

    number = jnp.int32(0)
    for s in range(arrays):
        kv[s, :, 0:prefix] = slots[s][...]
        kv[s, :, prefix:width] = own[...]
        lo, hi = starts[first + s], starts[first + s + 1]
        more = (hi - lo + BLOCK - 1) // BLOCK

        def note(b, _):
            blocks[0, number + b] = s
            blocks[1, number + b] = lo + b * BLOCK
            blocks[2, number + b] = jnp.minimum(lo + (b + 1) * BLOCK, hi)
            return 0

        lax.fori_loop(0, more, note, 0)
        number = number + more
    column = lax.broadcasted_iota(jnp.int32, (heads, width - prefix), 1)

    def score(b, to):
        begin = blocks[1, b]
        q = jnp.concatenate([query[order[begin + r]] for r in range(BLOCK)])
        to[...] = jnp.dot(q, kv[blocks[0, b]], preferred_element_type=jnp.float32)

    def finish(b, scores):
        begin = blocks[1, b]
        mine = [
            jnp.where(column == order[begin + r], scores[r * heads:(r + 1) * heads, prefix:width], -jnp.inf)
            for r in range(BLOCK)
        ]
        s = jnp.concatenate([scores[:, 0:prefix], jnp.concatenate(mine)], axis=1)
        top = jnp.max(s, axis=1, keepdims=True)
        expo = jnp.exp2((s - top) * (SCALE * math.log2(math.e)))
        total = jnp.sum(expo, axis=1, keepdims=True)
        weights = (expo * (1.0 / total)).astype(jnp.bfloat16)
        mixed = lax.dot_general(
            weights, kv[blocks[0, b], 0:LAT, :], (((1,), (1,)), ((), ())), preferred_element_type=jnp.float32
        )
        ov[pl.ds(begin, BLOCK)] = mixed.astype(jnp.bfloat16).reshape(BLOCK, heads, LAT)

    def send(b):
        @pl.loop(blocks[1, b], blocks[2, b])
        def _(j):
            pltpu.make_async_copy(ov.at[j], out.at[order[j]], out_sem).start()

    @pl.loop(0, number // 2)
    def _(pair):
        b = pair * 2
        score(b, even)
        score(b + 1, odd)
        finish(b, even)
        finish(b + 1, odd)
        if last:
            send(b)
            send(b + 1)

    @pl.when(number % 2 == 1)
    def _():
        score(number - 1, even)
        finish(number - 1, even)
        if last:
            send(number - 1)

    @pl.loop(from_row, to_row)
    def _(j):
        pltpu.make_async_copy(zeros, out.at[0], out_sem).wait()

    if last:

        @pl.loop(base, end)
        def _(j):
            pltpu.make_async_copy(zeros, out.at[0], out_sem).wait()


def attend(plan, first, query, own, slots, before=0, done=None, out=None, last=False, cost=COST):
    rows, heads, depth = query.shape
    count = len(slots)
    prefix = slots[0].shape[-1]
    width = prefix + own.shape[1]
    operands = [plan, query, own, *slots] + ([done, out] if before else [])
    work = rows * heads * count // (plan.shape[0] - BLOCK - rows - 1)
    result = jax.ShapeDtypeStruct((rows, heads, LAT), jnp.bfloat16)
    made = pltpu.VMEM((rows + BLOCK, heads, LAT), jnp.bfloat16)
    return pl.pallas_call(
        functools.partial(attend_kernel, first, before, last, count),
        out_shape=result if last else (result, made),
        in_specs=[SMEM, VMEM, VMEM] + [VMEM] * count + [VMEM, ANY] * (before > 0),
        out_specs=ANY if last else (ANY, VMEM),
        scratch_shapes=[made] * last + [
            pltpu.VMEM((count, depth, width), jnp.bfloat16),
            pltpu.VMEM((BLOCK * heads, width), jnp.float32),
            pltpu.VMEM((BLOCK * heads, width), jnp.float32),
            pltpu.VMEM((heads, LAT), jnp.bfloat16),
            pltpu.SMEM((3, rows // BLOCK + count + 4), jnp.int32),
            pltpu.SemaphoreType.DMA,
        ],
        input_output_aliases={len(operands) - 1: 0} if before else {},
        compiler_params=pltpu.CompilerParams(vmem_limit_bytes=16 * 1024 * 1024),
        cost_estimate=pl.CostEstimate(
            flops=cost * 2 * work * width * (depth + LAT),
            bytes_accessed=cost * (count * depth * width * 2 + work * LAT * 2),
            transcendentals=cost * work * width,
        ),
    )(*operands)


def ring_of(nodes):
    chips = nodes // 2
    if chips == 8:
        return [0, 2, 4, 6, 7, 5, 3, 1]
    return list(range(chips))


def shards(nodes, child_query, parent_cache, child_latent, parent_place, child_parent, live_rows):
    rows = child_query.shape[0]
    ring = ring_of(nodes)
    chips = len(ring)
    along = [(2 * ring[i], 2 * ring[(i + 1) % chips]) for i in range(chips)]
    along += [(2 * ring[(i + 1) % chips] + 1, 2 * ring[i] + 1) for i in range(chips)]
    across = [(i, i ^ 1) for i in range(nodes)]

    mine = jnp.swapaxes(parent_cache[0], 0, 1)
    other = lax.ppermute(mine, "node", across)
    other, place = lax.optimization_barrier((other, parent_place))
    plan, query, kept = prepare(place, jnp.swapaxes(child_parent, 0, 1), live_rows, child_query, mine)
    padded = -(-rows // 128) * 128
    pick = jnp.arange(rows)[:, None] == jnp.arange(padded)[None, :]
    own = lax.dot_general(
        child_latent, pick.astype(jnp.bfloat16), (((0,), (0,)), ((), ())), preferred_element_type=jnp.float32
    ).astype(jnp.bfloat16)

    first, result = 0, (None, None)
    phases = [[kept, other]]
    sent = [mine, other]

    def work(phase, last=False):
        nonlocal first, result
        before = len(phases[phase - 1]) if first else 0
        result = attend(plan, first, query, own, phases[phase], before, result[1], result[0], last, COST if first else FIRST)
        first += len(phases[phase])

    for i in range(1, chips):
        a = forward = lax.ppermute(sent[i - 1], "node", along)
        if i == 1:
            forward, plan = lax.optimization_barrier((a, plan))
        if i >= 2:
            if i == chips - 1:
                phases[i - 2].append(phases[i - 1].pop(0))
            work(i - 2)
            forward, done = lax.optimization_barrier((a, result[1]))
            result = result[0], done
        sent.append(forward)
        phases.append([a, lax.ppermute(forward, "node", across)])
    phases[-2].append(phases[-1].pop(0))
    work(chips - 2)
    work(chips - 1, True)
    return result


def solution(mesh):
    return jax.shard_map(
        functools.partial(shards, mesh.shape["node"]),
        mesh=mesh,
        in_specs=(
            P(("groups", "node"), None, None),
            P(("groups", "node"), None, None),
            P(("groups", "node"), None),
            P("groups"),
            P(("groups", "node"), None),
            P(("groups", "node")),
        ),
        out_specs=P(("groups", "node"), None, None),
        check_vma=False,
    )
```

```python
import functools
import math

import jax
import jax.numpy as jnp
from jax import lax
from jax.experimental import pallas as pl
from jax.experimental.pallas import tpu as pltpu
from jax.sharding import PartitionSpec as P

LAT = 512
SCALE = 0.07216878364870322
BLOCK = 6
COST = 4
FIRST = 1
ANY = pl.BlockSpec(memory_space=pl.ANY)
VMEM = pl.BlockSpec(memory_space=pltpu.VMEM)
SMEM = pl.BlockSpec(memory_space=pltpu.SMEM)


def position_of(chip, chips):
    if chips == 8:
        return jnp.where(chip % 2 == 0, chip // 2, 7 - chip // 2)
    return chip


def slot_of(ahead, same, chips):
    far = jnp.minimum(ahead, chips - ahead)
    slot = 4 * far - 2 + jnp.where(2 * ahead > chips, jnp.where(same, 0, 2), jnp.where(same, 3, 1))
    slot = jnp.where(2 * ahead == chips, 4 * far - 2 + jnp.where(same, 0, 1), slot)
    return jnp.where(ahead == 0, jnp.where(same, 0, 1), slot)


def prepare_kernel(
    place_in, parent_in, live_in, query_in, mine_in, plan, query, mine, place, parent, live, slots, names, starts, sem
):
    rows = parent.shape[1]
    parents = place.shape[0]
    dead = starts.shape[0] - 1
    chips = parents // 2
    big = [
        pltpu.make_async_copy(query_in, query, sem.at[0]),
        pltpu.make_async_copy(mine_in, mine, sem.at[1]),
    ]
    small = [
        pltpu.make_async_copy(place_in, place, sem.at[2]),
        pltpu.make_async_copy(parent_in, parent, sem.at[3]),
        pltpu.make_async_copy(live_in, live, sem.at[4]),
    ]
    for copy in small + big:
        copy.start()
    for copy in small:
        copy.wait()
    me = lax.axis_index("node")
    core = me % 2
    here = position_of(me // 2, chips)
    alive = live[0]

    def name(p, _):
        at = place[p]
        there = position_of(at // 2, chips)
        ahead = jnp.where(core == 0, there - here, here - there)
        ahead = jnp.where(ahead < 0, ahead + chips, ahead)
        names[p] = slot_of(ahead, at % 2 == core, chips)
        starts[p] = 0
        return 0

    lax.fori_loop(0, parents, name, 0, unroll=4)
    starts[dead] = 0

    def tally(i, _):
        s = jnp.where(i < alive, names[parent[0, i]], dead)
        slots[i] = s
        starts[s] = starts[s] + 1
        return 0

    lax.fori_loop(0, rows, tally, 0, unroll=8)

    def ends(s, total):
        total = total + starts[s]
        starts[s] = total
        return total

    lax.fori_loop(0, dead + 1, ends, jnp.int32(0))

    def put(i, _):
        i = rows - 1 - i
        s = slots[i]
        j = starts[s] - 1
        starts[s] = j
        plan[dead + 1 + j] = i
        return 0

    lax.fori_loop(0, rows, put, 0, unroll=8)
    for i in range(dead + 1 + rows, plan.shape[0]):
        plan[i] = 0

    def tell(s, _):
        plan[s] = starts[s]
        return 0

    lax.fori_loop(0, dead + 1, tell, 0)
    for copy in big:
        copy.wait()


def prepare(place, parent, live, query, mine):
    rows, parents = parent.shape[1], place.shape[0]
    return pl.pallas_call(
        prepare_kernel,
        out_shape=(
            jax.ShapeDtypeStruct((parents + 1 + rows + BLOCK,), jnp.int32),
            pltpu.VMEM(query.shape, query.dtype),
            pltpu.VMEM(mine.shape, mine.dtype),
        ),
        in_specs=[ANY] * 5,
        out_specs=(SMEM, VMEM, VMEM),
        scratch_shapes=[
            pltpu.SMEM(place.shape, jnp.int32),
            pltpu.SMEM(parent.shape, jnp.int32),
            pltpu.SMEM(live.shape, jnp.int32),
            pltpu.SMEM((rows,), jnp.int32),
            pltpu.SMEM(place.shape, jnp.int32),
            pltpu.SMEM((parents + 1,), jnp.int32),
            pltpu.SemaphoreType.DMA((5,)),
        ],
        compiler_params=pltpu.CompilerParams(vmem_limit_bytes=48 * 1024 * 1024),
        cost_estimate=pl.CostEstimate(flops=0, bytes_accessed=2 * query.size * 2, transcendentals=0),
    )(place, parent, live, query, mine)


def attend_kernel(first, before, last, arrays, plan, query, own, *refs):
    slots = refs[:arrays]
    out, ov, kv, even, odd, zeros, blocks, out_sem = refs[-8:]
    done = refs[arrays] if before else None
    rows, heads, depth = query.shape
    prefix = slots[0].shape[-1]
    block = even.shape[0] // heads
    width = kv.shape[2]
    dead = plan.shape[0] - BLOCK - rows - 1
    order = plan.at[pl.ds(dead + 1, rows + BLOCK)]
    starts = plan.at[pl.ds(0, dead + 1)]
    base = starts[first]
    end = starts[first + arrays]

    if before:
        from_row, to_row = starts[first - before], base
    else:
        zeros[...] = jnp.zeros_like(zeros)
        from_row, to_row = starts[dead], rows

    @pl.loop(from_row, to_row)
    def _(j):
        pltpu.make_async_copy(done.at[j] if before else zeros, out.at[order[j]], out_sem).start()

    number = jnp.int32(0)
    for s in range(arrays):
        kv[s, :, 0:prefix] = slots[s][...]
        kv[s, :, prefix:width] = own[...]
        lo, hi = starts[first + s], starts[first + s + 1]
        more = (hi - lo + block - 1) // block

        def note(b, _):
            blocks[0, number + b] = s
            blocks[1, number + b] = lo + b * block
            blocks[2, number + b] = jnp.minimum(lo + (b + 1) * block, hi)
            return 0

        lax.fori_loop(0, more, note, 0)
        number = number + more
    column = lax.broadcasted_iota(jnp.int32, (heads, width - prefix), 1)

    def score(b, to):
        begin = blocks[1, b]
        q = jnp.concatenate([query[order[begin + r]] for r in range(block)])
        to[...] = jnp.dot(q, kv[blocks[0, b]], preferred_element_type=jnp.float32)

    def finish(b, scores):
        begin = blocks[1, b]
        mine = [
            jnp.where(column == order[begin + r], scores[r * heads:(r + 1) * heads, prefix:width], -jnp.inf)
            for r in range(block)
        ]
        s = jnp.concatenate([scores[:, 0:prefix], jnp.concatenate(mine)], axis=1)
        top = jnp.max(s, axis=1, keepdims=True)
        expo = jnp.exp2((s - top) * (SCALE * math.log2(math.e)))
        total = jnp.sum(expo, axis=1, keepdims=True)
        weights = (expo * (1.0 / total)).astype(jnp.bfloat16)
        mixed = lax.dot_general(
            weights, kv[blocks[0, b], 0:LAT, :], (((1,), (1,)), ((), ())), preferred_element_type=jnp.float32
        )
        ov[pl.ds(begin, block)] = mixed.astype(jnp.bfloat16).reshape(block, heads, LAT)

    def send(b):
        @pl.loop(blocks[1, b], blocks[2, b])
        def _(j):
            pltpu.make_async_copy(ov.at[j], out.at[order[j]], out_sem).start()

    @pl.loop(0, number // 2)
    def _(pair):
        b = pair * 2
        score(b, even)
        score(b + 1, odd)
        finish(b, even)
        finish(b + 1, odd)
        if last:
            send(b)
            send(b + 1)

    @pl.when(number % 2 == 1)
    def _():
        score(number - 1, even)
        finish(number - 1, even)
        if last:
            send(number - 1)

    @pl.loop(from_row, to_row)
    def _(j):
        pltpu.make_async_copy(zeros, out.at[0], out_sem).wait()

    if last:

        @pl.loop(base, end)
        def _(j):
            pltpu.make_async_copy(zeros, out.at[0], out_sem).wait()


def attend(plan, first, query, own, slots, before=0, done=None, out=None, last=False, cost=COST):
    rows, heads, depth = query.shape
    count = len(slots)
    block = BLOCK // 2 if last else BLOCK
    prefix = slots[0].shape[-1]
    width = prefix + own.shape[1]
    operands = [plan, query, own, *slots] + ([done, out] if before else [])
    work = rows * heads * count // (plan.shape[0] - BLOCK - rows - 1)
    result = jax.ShapeDtypeStruct((rows, heads, LAT), jnp.bfloat16)
    made = pltpu.VMEM((rows + BLOCK, heads, LAT), jnp.bfloat16)
    return pl.pallas_call(
        functools.partial(attend_kernel, first, before, last, count),
        out_shape=result if last else (result, made),
        in_specs=[SMEM, VMEM, VMEM] + [VMEM] * count + [VMEM, ANY] * (before > 0),
        out_specs=ANY if last else (ANY, VMEM),
        scratch_shapes=[made] * last + [
            pltpu.VMEM((count, depth, width), jnp.bfloat16),
            pltpu.VMEM((block * heads, width), jnp.float32),
            pltpu.VMEM((block * heads, width), jnp.float32),
            pltpu.VMEM((heads, LAT), jnp.bfloat16),
            pltpu.SMEM((3, rows // block + count + 4), jnp.int32),
            pltpu.SemaphoreType.DMA,
        ],
        input_output_aliases={len(operands) - 1: 0} if before else {},
        compiler_params=pltpu.CompilerParams(vmem_limit_bytes=16 * 1024 * 1024),
        cost_estimate=pl.CostEstimate(
            flops=cost * 2 * work * width * (depth + LAT),
            bytes_accessed=cost * (count * depth * width * 2 + work * LAT * 2),
            transcendentals=cost * work * width,
        ),
    )(*operands)


def ring_of(nodes):
    chips = nodes // 2
    if chips == 8:
        return [0, 2, 4, 6, 7, 5, 3, 1]
    return list(range(chips))


def shards(nodes, child_query, parent_cache, child_latent, parent_place, child_parent, live_rows):
    rows = child_query.shape[0]
    ring = ring_of(nodes)
    chips = len(ring)
    along = [(2 * ring[i], 2 * ring[(i + 1) % chips]) for i in range(chips)]
    along += [(2 * ring[(i + 1) % chips] + 1, 2 * ring[i] + 1) for i in range(chips)]
    across = [(i, i ^ 1) for i in range(nodes)]

    mine = jnp.swapaxes(parent_cache[0], 0, 1)
    other = lax.ppermute(mine, "node", across)
    other, place = lax.optimization_barrier((other, parent_place))
    plan, query, kept = prepare(place, jnp.swapaxes(child_parent, 0, 1), live_rows, child_query, mine)
    padded = -(-rows // 128) * 128
    pick = jnp.arange(rows)[:, None] == jnp.arange(padded)[None, :]
    own = lax.dot_general(
        child_latent, pick.astype(jnp.bfloat16), (((0,), (0,)), ((), ())), preferred_element_type=jnp.float32
    ).astype(jnp.bfloat16)

    first, result = 0, (None, None)
    phases = [[kept, other]]
    sent = [mine, other]

    def work(phase, last=False):
        nonlocal first, result
        before = len(phases[phase - 1]) if first else 0
        result = attend(plan, first, query, own, phases[phase], before, result[1], result[0], last, COST if first else FIRST)
        first += len(phases[phase])

    for i in range(1, chips):
        a = forward = lax.ppermute(sent[i - 1], "node", along)
        if i == 1:
            forward, plan = lax.optimization_barrier((a, plan))
        if i >= 2:
            if i == chips - 1:
                phases[i - 2].append(phases[i - 1].pop(0))
            work(i - 2)
            forward, done = lax.optimization_barrier((a, result[1]))
            result = result[0], done
        sent.append(forward)
        phases.append([a, lax.ppermute(forward, "node", across)])
    phases[-2].append(phases[-1].pop(0))
    work(chips - 2)
    work(chips - 1, True)
    return result


def solution(mesh):
    return jax.shard_map(
        functools.partial(shards, mesh.shape["node"]),
        mesh=mesh,
        in_specs=(
            P(("groups", "node"), None, None),
            P(("groups", "node"), None, None),
            P(("groups", "node"), None),
            P("groups"),
            P(("groups", "node"), None),
            P(("groups", "node")),
        ),
        out_specs=P(("groups", "node"), None, None),
        check_vma=False,
    )
```

```python
import functools
import math

import jax
import jax.numpy as jnp
from jax import lax
from jax.experimental import pallas as pl
from jax.experimental.pallas import tpu as pltpu
from jax.sharding import PartitionSpec as P

LAT = 512
SCALE = 0.07216878364870322
BLOCK = 6
COST = 4
FIRST = 1
ANY = pl.BlockSpec(memory_space=pl.ANY)
VMEM = pl.BlockSpec(memory_space=pltpu.VMEM)
SMEM = pl.BlockSpec(memory_space=pltpu.SMEM)


def position_of(chip, chips):
    if chips == 8:
        return jnp.where(chip % 2 == 0, chip // 2, 7 - chip // 2)
    return chip


def slot_of(ahead, same, chips):
    far = jnp.minimum(ahead, chips - ahead)
    slot = 4 * far - 2 + jnp.where(2 * ahead > chips, jnp.where(same, 0, 2), jnp.where(same, 3, 1))
    slot = jnp.where(2 * ahead == chips, 4 * far - 2 + jnp.where(same, 0, 1), slot)
    return jnp.where(ahead == 0, jnp.where(same, 0, 1), slot)


def prepare_kernel(
    place_in, parent_in, live_in, query_in, mine_in, plan, query, mine, place, parent, live, slots, names, starts, sem
):
    rows = parent.shape[1]
    parents = place.shape[0]
    dead = starts.shape[0] - 1
    chips = parents // 2
    big = [
        pltpu.make_async_copy(query_in, query, sem.at[0]),
        pltpu.make_async_copy(mine_in, mine, sem.at[1]),
    ]
    small = [
        pltpu.make_async_copy(place_in, place, sem.at[2]),
        pltpu.make_async_copy(parent_in, parent, sem.at[3]),
        pltpu.make_async_copy(live_in, live, sem.at[4]),
    ]
    for copy in small + big:
        copy.start()
    for copy in small:
        copy.wait()
    me = lax.axis_index("node")
    core = me % 2
    here = position_of(me // 2, chips)
    alive = live[0]

    def name(p, _):
        at = place[p]
        there = position_of(at // 2, chips)
        ahead = jnp.where(core == 0, there - here, here - there)
        ahead = jnp.where(ahead < 0, ahead + chips, ahead)
        names[p] = slot_of(ahead, at % 2 == core, chips)
        starts[p] = 0
        return 0

    lax.fori_loop(0, parents, name, 0, unroll=4)
    starts[dead] = 0

    def tally(i, _):
        s = jnp.where(i < alive, names[parent[0, i]], dead)
        slots[i] = s
        starts[s] = starts[s] + 1
        return 0

    lax.fori_loop(0, rows, tally, 0, unroll=8)

    def ends(s, total):
        total = total + starts[s]
        starts[s] = total
        return total

    lax.fori_loop(0, dead + 1, ends, jnp.int32(0))

    def put(i, _):
        i = rows - 1 - i
        s = slots[i]
        j = starts[s] - 1
        starts[s] = j
        plan[dead + 1 + j] = i
        return 0

    lax.fori_loop(0, rows, put, 0, unroll=8)
    for i in range(dead + 1 + rows, plan.shape[0]):
        plan[i] = 0

    def tell(s, _):
        plan[s] = starts[s]
        return 0

    lax.fori_loop(0, dead + 1, tell, 0)
    for copy in big:
        copy.wait()


def prepare(place, parent, live, query, mine):
    rows, parents = parent.shape[1], place.shape[0]
    return pl.pallas_call(
        prepare_kernel,
        out_shape=(
            jax.ShapeDtypeStruct((parents + 1 + rows + BLOCK,), jnp.int32),
            pltpu.VMEM(query.shape, query.dtype),
            pltpu.VMEM(mine.shape, mine.dtype),
        ),
        in_specs=[ANY] * 5,
        out_specs=(SMEM, VMEM, VMEM),
        scratch_shapes=[
            pltpu.SMEM(place.shape, jnp.int32),
            pltpu.SMEM(parent.shape, jnp.int32),
            pltpu.SMEM(live.shape, jnp.int32),
            pltpu.SMEM((rows,), jnp.int32),
            pltpu.SMEM(place.shape, jnp.int32),
            pltpu.SMEM((parents + 1,), jnp.int32),
            pltpu.SemaphoreType.DMA((5,)),
        ],
        compiler_params=pltpu.CompilerParams(vmem_limit_bytes=48 * 1024 * 1024),
        cost_estimate=pl.CostEstimate(flops=0, bytes_accessed=2 * query.size * 2, transcendentals=0),
    )(place, parent, live, query, mine)


def attend_kernel(first, before, last, arrays, plan, query, own, *refs):
    slots = refs[:arrays]
    out, ov, kv, even, odd, zeros, blocks, out_sem = refs[-8:]
    done = refs[arrays] if before else None
    rows, heads, depth = query.shape
    prefix = slots[0].shape[-1]
    width = kv.shape[2]
    dead = plan.shape[0] - BLOCK - rows - 1
    order = plan.at[pl.ds(dead + 1, rows + BLOCK)]
    starts = plan.at[pl.ds(0, dead + 1)]
    base = starts[first]
    end = starts[first + arrays]

    if before:
        from_row, to_row = starts[first - before], base
    else:
        zeros[...] = jnp.zeros_like(zeros)
        from_row, to_row = starts[dead], rows

    @pl.loop(from_row, to_row)
    def _(j):
        pltpu.make_async_copy(done.at[j] if before else zeros, out.at[order[j]], out_sem).start()

    number = jnp.int32(0)
    for s in range(arrays):
        kv[s, :, 0:prefix] = slots[s][...]
        kv[s, :, prefix:width] = own[...]
        lo, hi = starts[first + s], starts[first + s + 1]
        more = (hi - lo + BLOCK - 1) // BLOCK

        def note(b, _):
            blocks[0, number + b] = s
            blocks[1, number + b] = lo + b * BLOCK
            blocks[2, number + b] = jnp.minimum(lo + (b + 1) * BLOCK, hi)
            return 0

        lax.fori_loop(0, more, note, 0)
        number = number + more
    column = lax.broadcasted_iota(jnp.int32, (heads, width - prefix), 1)

    def score(b, to):
        begin = blocks[1, b]
        q = jnp.concatenate([query[order[begin + r]] for r in range(BLOCK)])
        to[...] = jnp.dot(q, kv[blocks[0, b]], preferred_element_type=jnp.float32)

    def finish(b, scores):
        begin = blocks[1, b]
        mine = [
            jnp.where(column == order[begin + r], scores[r * heads:(r + 1) * heads, prefix:width], -jnp.inf)
            for r in range(BLOCK)
        ]
        s = jnp.concatenate([scores[:, 0:prefix], jnp.concatenate(mine)], axis=1)
        top = jnp.max(s, axis=1, keepdims=True)
        expo = jnp.exp2((s - top) * (SCALE * math.log2(math.e)))
        total = jnp.sum(expo, axis=1, keepdims=True)
        weights = (expo * (1.0 / total)).astype(jnp.bfloat16)
        mixed = lax.dot_general(
            weights, kv[blocks[0, b], 0:LAT, :], (((1,), (1,)), ((), ())), preferred_element_type=jnp.float32
        )
        ov[pl.ds(begin, BLOCK)] = mixed.astype(jnp.bfloat16).reshape(BLOCK, heads, LAT)

    def send(b):
        @pl.loop(blocks[1, b], blocks[2, b])
        def _(j):
            pltpu.make_async_copy(ov.at[j], out.at[order[j]], out_sem).start()

    @pl.loop(0, number // 2)
    def _(pair):
        b = pair * 2
        score(b, even)
        score(b + 1, odd)
        finish(b, even)
        if last:
            send(b)
        finish(b + 1, odd)
        if last:
            send(b + 1)

    @pl.when(number % 2 == 1)
    def _():
        score(number - 1, even)
        finish(number - 1, even)
        if last:
            send(number - 1)

    @pl.loop(from_row, to_row)
    def _(j):
        pltpu.make_async_copy(zeros, out.at[0], out_sem).wait()

    if last:

        @pl.loop(base, end)
        def _(j):
            pltpu.make_async_copy(zeros, out.at[0], out_sem).wait()


def attend(plan, first, query, own, slots, before=0, done=None, out=None, last=False, cost=COST):
    rows, heads, depth = query.shape
    count = len(slots)
    prefix = slots[0].shape[-1]
    width = prefix + own.shape[1]
    operands = [plan, query, own, *slots] + ([done, out] if before else [])
    work = rows * heads * count // (plan.shape[0] - BLOCK - rows - 1)
    result = jax.ShapeDtypeStruct((rows, heads, LAT), jnp.bfloat16)
    made = pltpu.VMEM((rows + BLOCK, heads, LAT), jnp.bfloat16)
    return pl.pallas_call(
        functools.partial(attend_kernel, first, before, last, count),
        out_shape=result if last else (result, made),
        in_specs=[SMEM, VMEM, VMEM] + [VMEM] * count + [VMEM, ANY] * (before > 0),
        out_specs=ANY if last else (ANY, VMEM),
        scratch_shapes=[made] * last + [
            pltpu.VMEM((count, depth, width), jnp.bfloat16),
            pltpu.VMEM((BLOCK * heads, width), jnp.float32),
            pltpu.VMEM((BLOCK * heads, width), jnp.float32),
            pltpu.VMEM((heads, LAT), jnp.bfloat16),
            pltpu.SMEM((3, rows // BLOCK + count + 4), jnp.int32),
            pltpu.SemaphoreType.DMA,
        ],
        input_output_aliases={len(operands) - 1: 0} if before else {},
        compiler_params=pltpu.CompilerParams(vmem_limit_bytes=16 * 1024 * 1024),
        cost_estimate=pl.CostEstimate(
            flops=cost * 2 * work * width * (depth + LAT),
            bytes_accessed=cost * (count * depth * width * 2 + work * LAT * 2),
            transcendentals=cost * work * width,
        ),
    )(*operands)


def ring_of(nodes):
    chips = nodes // 2
    if chips == 8:
        return [0, 2, 4, 6, 7, 5, 3, 1]
    return list(range(chips))


def shards(nodes, child_query, parent_cache, child_latent, parent_place, child_parent, live_rows):
    rows = child_query.shape[0]
    ring = ring_of(nodes)
    chips = len(ring)
    along = [(2 * ring[i], 2 * ring[(i + 1) % chips]) for i in range(chips)]
    along += [(2 * ring[(i + 1) % chips] + 1, 2 * ring[i] + 1) for i in range(chips)]
    across = [(i, i ^ 1) for i in range(nodes)]

    mine = jnp.swapaxes(parent_cache[0], 0, 1)
    other = lax.ppermute(mine, "node", across)
    other, place = lax.optimization_barrier((other, parent_place))
    plan, query, kept = prepare(place, jnp.swapaxes(child_parent, 0, 1), live_rows, child_query, mine)
    padded = -(-rows // 128) * 128
    pick = jnp.arange(rows)[:, None] == jnp.arange(padded)[None, :]
    own = lax.dot_general(
        child_latent, pick.astype(jnp.bfloat16), (((0,), (0,)), ((), ())), preferred_element_type=jnp.float32
    ).astype(jnp.bfloat16)

    first, result = 0, (None, None)
    phases = [[kept, other]]
    sent = [mine, other]

    def work(phase, last=False):
        nonlocal first, result
        before = len(phases[phase - 1]) if first else 0
        result = attend(plan, first, query, own, phases[phase], before, result[1], result[0], last, COST if first else FIRST)
        first += len(phases[phase])

    for i in range(1, chips):
        a = forward = lax.ppermute(sent[i - 1], "node", along)
        if i == 1:
            forward, plan = lax.optimization_barrier((a, plan))
        if i >= 2:
            if i == chips - 1:
                phases[i - 2].append(phases[i - 1].pop(0))
            work(i - 2)
            forward, done = lax.optimization_barrier((a, result[1]))
            result = result[0], done
        sent.append(forward)
        phases.append([a, lax.ppermute(forward, "node", across)])
    phases[-2].append(phases[-1].pop(0))
    work(chips - 2)
    work(chips - 1, True)
    return result


def solution(mesh):
    return jax.shard_map(
        functools.partial(shards, mesh.shape["node"]),
        mesh=mesh,
        in_specs=(
            P(("groups", "node"), None, None),
            P(("groups", "node"), None, None),
            P(("groups", "node"), None),
            P("groups"),
            P(("groups", "node"), None),
            P(("groups", "node")),
        ),
        out_specs=P(("groups", "node"), None, None),
        check_vma=False,
    )
```
